128 devices in a mesh: row: 8 (over x_hi, z), col: 16 (over y, x_lo, core).
Axes of the slice: x: 4 (x_hi: 2, x_lo: 2; x = x_hi * 2 + x_lo), y: 4, z: 4, core: 2. Of those that a mesh axis runs over, the one named last changes fastest.
Arguments:
- seq: bfloat16 [3072, 1024], P(('row', 'col')), may hold values from -6 to 6
- gain: float32 [1024], replicated, may hold values from 0.5 to 1.5
- beta: float32 [1024], replicated, may hold values from -3 to 3
- w_proj: bfloat16 [1024, 128], replicated, may hold values from -0.1875 to 0.1875
- b_proj: float32 [128], replicated, may hold values from -3 to 3
- w_out: bfloat16 [128, 128], replicated, may hold values from -0.5 to 0.5
- pair_grad: bfloat16 [3072, 3072, 128], P('row', 'col'), may hold values from -0.059814453 to 0.059814453
Outputs:
- d_seq: bfloat16 [3072, 1024], P(('row', 'col'))
- d_w_proj: float32 [1024, 128], replicated
- d_b_proj: float32 [128], replicated
- d_w_out: float32 [128, 128], replicated
- d_b_out: float32 [128], replicated
The draws below stay inside these ranges and needn't reach their ends.
All inputs are finite; a program needn't handle non-finite values.
Results may differ from the reference program's by a relative error of at most 0.0065.
Values may be sent and summed in bfloat16 or wider, within the bound.
No kernel may reach another device: no remote copies, remote signals or barrier semaphores. Data moves between devices by JAX's collectives and lax.ppermute only.
A program may use at most 128 MiB of HBM per device.

```python
import jax
import jax.numpy as jnp
from jax import lax

SEQ_D = 1024
INNER = 64
PAIR = 128
RES = 3072
N_ROW = 8


def shard_levels(key, dims, cuts, smallest, largest):
    loudness = 1.0
    for dim, parts in cuts:
        heights = jax.random.uniform(jax.random.fold_in(jax.random.fold_in(key, 6), dim), (parts,), jnp.float32, smallest / len(cuts), largest / len(cuts))
        loudness = loudness * jnp.repeat(jnp.exp(heights), dims[dim] // parts).reshape((-1,) + (1,) * (len(dims) - 1 - dim))
    return loudness


def noise(own_key, shape, width, bound, shards=(), held_as=jnp.bfloat16):
    level = shard_levels(own_key, shape, shards, -0.22, 0.18) if shards else 1.0
    drawn = jax.random.normal(own_key, shape, jnp.float32) * width * level
    return jnp.minimum(jnp.maximum(drawn, -bound), bound).astype(held_as)


def setup_inputs(seed: int = 0) -> dict:
    seeds = jax.random.split(jax.random.key(seed), 8)
    return {
        "seq": noise(seeds[0], (RES, SEQ_D), 1.0, 6.0, ((0, 128),)),
        "gain": jnp.clip(1.0 + 0.1 * jax.random.normal(seeds[1], (SEQ_D,), jnp.float32), 0.5, 1.5),
        "beta": noise(seeds[2], (SEQ_D,), 0.5, 3.0, (), jnp.float32),
        "w_proj": noise(seeds[3], (SEQ_D, 2 * INNER), SEQ_D ** -0.5, 0.1875),
        "b_proj": noise(seeds[4], (2 * INNER,), 0.5, 3.0, (), jnp.float32),
        "w_out": noise(seeds[5], (2 * INNER, PAIR), (2 * INNER) ** -0.5, 0.5),
        "pair_grad": noise(seeds[6], (RES, RES, PAIR), 0.01, 0.059814453, ((0, 8), (1, 16))),
    }


def reference(seq, gain, beta, w_proj, b_proj, w_out, pair_grad):
    source = seq.astype(jnp.float32)
    mean_val = lax.optimization_barrier(jnp.mean(source, axis=1, keepdims=True))
    centred = source - mean_val
    variance = lax.optimization_barrier(jnp.mean(centred * centred, axis=1, keepdims=True))
    inverse = 1.0 / jnp.sqrt(variance + 1e-05)
    normed = centred * inverse
    y_rows = (normed * gain + beta).astype(jnp.bfloat16)
    qk_rows = (jnp.dot(y_rows, w_proj, preferred_element_type=jnp.float32) + b_proj).astype(jnp.bfloat16)
    query = qk_rows[:, :INNER].astype(jnp.float32)
    key_rows = qk_rows[:, INNER:].astype(jnp.float32)
    ones_half = jnp.ones((RES, INNER), jnp.float32)
    key_ext = jnp.concatenate([key_rows, ones_half], axis=1)
    key_twice = jnp.concatenate([key_rows, key_rows], axis=1)
    query_ext = jnp.concatenate([query, -ones_half], axis=1)
    query_twice = jnp.concatenate([query, query], axis=1)
    lanes = jnp.arange(2 * INNER) < INNER
    block = RES // N_ROW
    wout_f = w_out.astype(jnp.float32)

    def step(carry, inputs):
        key_acc, wout_acc, bout_acc = carry
        grad_blk, qext_blk, qtwo_blk = inputs
        grad_f = grad_blk.astype(jnp.float32)
        big_g = jnp.einsum('ijp,cp->ijc', grad_f, wout_f)
        part = jnp.einsum('ijc,jc->ic', big_g, key_ext)
        dq_blk = part[:, :INNER] + part[:, INNER:]
        key_acc = key_acc + jnp.einsum('ijc,ic->jc', big_g, qext_blk)
        feats = jnp.where(lanes, qtwo_blk[:, None, :] * key_twice[None, :, :], qtwo_blk[:, None, :] - key_twice[None, :, :])
        feats = feats.astype(jnp.bfloat16).astype(jnp.float32)
        wout_acc = wout_acc + jnp.einsum('ijc,ijp->cp', feats, grad_f)
        bout_acc = bout_acc + lax.optimization_barrier(jnp.sum(grad_f, axis=(0, 1)))
        return ((key_acc, wout_acc, bout_acc), dq_blk)
    init = (jnp.zeros((RES, 2 * INNER), jnp.float32), jnp.zeros((2 * INNER, PAIR), jnp.float32), jnp.zeros((PAIR,), jnp.float32))
    inputs = (pair_grad.reshape(N_ROW, block, RES, PAIR), query_ext.reshape(N_ROW, block, 2 * INNER), query_twice.reshape(N_ROW, block, 2 * INNER))
    (key_acc, d_w_out, d_b_out), dq_blocks = lax.scan(step, init, inputs)
    dq_all = dq_blocks.reshape(RES, INNER)
    dk_all = key_acc[:, :INNER] + key_acc[:, INNER:]
    dqk = jnp.concatenate([dq_all, dk_all], axis=1)
    d_b_proj = lax.optimization_barrier(jnp.sum(dqk, axis=0))
    dqk_b = dqk.astype(jnp.bfloat16)
    d_w_proj = jnp.dot(y_rows.T, dqk_b, preferred_element_type=jnp.float32)
    d_normed = jnp.dot(dqk_b, w_proj.T, preferred_element_type=jnp.float32) * gain
    d_seq = inverse * (d_normed - lax.optimization_barrier(jnp.mean(d_normed, axis=1, keepdims=True)) - normed * lax.optimization_barrier(jnp.mean(d_normed * normed, axis=1, keepdims=True)))
    return (d_seq.astype(jnp.bfloat16), d_w_proj, d_b_proj, d_w_out, d_b_out)
```

```python
import functools

import jax
import jax.numpy as jnp
from jax import lax
from jax.experimental import pallas as pl
from jax.experimental.pallas import tpu as pltpu
from jax.sharding import PartitionSpec as P

F32 = jnp.float32
BF16 = jnp.bfloat16
BOTH = ("row", "col")
CHUNK = 32


def _params(mib):
    return pltpu.CompilerParams(vmem_limit_bytes=mib * 2**20)


def _vmem(n):
    return [pl.BlockSpec(memory_space=pltpu.VMEM)] * n


def _norm(seq):
    source = seq.astype(F32)
    centred = source - jnp.mean(source, axis=1, keepdims=True)
    variance = jnp.mean(centred * centred, axis=1, keepdims=True)
    inverse = 1.0 / jnp.sqrt(variance + 1e-05)
    return centred * inverse, inverse


def _project_kernel(seq_ref, gain_ref, beta_ref, w_ref, b_ref, out_ref):
    normed, _ = _norm(seq_ref[...])
    y = (normed * gain_ref[...] + beta_ref[...]).astype(BF16)
    qk = (jnp.dot(y, w_ref[...], preferred_element_type=F32) + b_ref[...]).astype(BF16)
    out_ref[...] = jnp.broadcast_to(qk[None], out_ref.shape)


def _pair_kernel(
    qk_ref, w_ref, pg_hbm, dq_ref, dk_ref, dw_ref, db_ref,
    pg, sems, q2_s, qt_s, kt_s, k2_s, wbd_s, dq_s, r_s, dk_s, dwp_s, s_s,
):
    rows, cols, pair = pg.shape
    inner = pair // 2
    half = cols // 2
    n_chunks = rows // CHUNK

    def copy(ch):
        part = pl.ds(ch * CHUNK, CHUNK)
        return pltpu.make_async_copy(pg_hbm.at[part], pg.at[part], sems.at[ch])

    for ch in range(n_chunks):
        copy(ch).start()

    nq, shard = dq_ref.shape[0], dq_ref.shape[1]
    nk = dk_ref.shape[0]
    me_r = lax.axis_index("row")
    me_c = lax.axis_index("col")
    q = qk_ref[pl.ds(me_r * nq, nq)].astype(F32).reshape(rows, pair)[:, :inner]
    k = qk_ref[pl.ds(me_c * nk, nk)].astype(F32).reshape(cols, pair)[:, inner:]
    q2_s[...] = jnp.concatenate([q, q], axis=1)
    k2_s[...] = jnp.concatenate([k[:half], k[half:]], axis=1)
    qt = q.T
    for ch in range(n_chunks):
        qt_s[ch] = qt[:, ch * CHUNK : (ch + 1) * CHUNK]
    kt_s[...] = jnp.concatenate([k.T, jnp.ones((16, cols), F32)], axis=0).astype(BF16)
    wt = w_ref[...].astype(F32).T
    blank = jnp.zeros((pair, inner), F32)
    top = jnp.concatenate([wt[:, :inner], blank, wt[:, inner:], blank], axis=1)
    bottom = jnp.concatenate([blank, wt[:, :inner], blank, wt[:, inner:]], axis=1)
    wbd_s[...] = jnp.concatenate([top, bottom], axis=0).astype(BF16)
    dk_s[...] = jnp.zeros_like(dk_s)
    dwp_s[...] = jnp.zeros_like(dwp_s)
    s_s[...] = jnp.zeros_like(s_s)

    def chunk(ch, carry):
        copy(ch).wait()
        base = ch * CHUNK
        dk = dk_s[...]
        k2 = k2_s[...]
        for i in range(CHUNK):
            block = pg[base + i]
            g = jnp.dot(
                jnp.concatenate([block[:half], block[half:]], axis=1),
                wbd_s[...],
                preferred_element_type=F32,
            )
            gp, gd = g[:, :pair], g[:, pair:]
            dq_s[pl.ds(base + i, 1), :] = jnp.sum(gp * k2 + gd, axis=0, keepdims=True)
            dk = dk + (gp * q2_s[pl.ds(base + i, 1), :] - gd)
        dk_s[...] = dk
        dwp = dwp_s[...]
        s = s_s[...]
        for i in range(0, CHUNK, 2):
            a = jnp.dot(
                kt_s[...],
                jnp.concatenate([pg[base + i], pg[base + i + 1]], axis=1),
                preferred_element_type=F32,
            )
            a0, a1 = a[:inner, :pair], a[:inner, pair:]
            dwp = dwp + (a0 * qt_s[ch, :, i : i + 1] + a1 * qt_s[ch, :, i + 1 : i + 2])
            s = s + (a0 + a1)
            r_s[pl.ds(base + i, 1), :] = a[inner : inner + 1, :pair]
            r_s[pl.ds(base + i + 1, 1), :] = a[inner : inner + 1, pair:]
        dwp_s[...] = dwp
        s_s[...] = s
        return carry

    lax.fori_loop(0, n_chunks, chunk, 0)

    dq = dq_s[...]
    dq = dq[:, :inner] + dq[:, inner:]
    dq_ref[...] = jnp.concatenate([dq, jnp.zeros_like(dq)], axis=1).reshape(dq_ref.shape)
    dk = dk_s[...]
    dk = jnp.concatenate([dk[:, :inner], dk[:, inner:]], axis=0)
    dk_ref[...] = jnp.concatenate([dk, jnp.zeros_like(dk)], axis=1).reshape(dk_ref.shape)
    r = r_s[...]
    dw_ref[:inner, :] = dwp_s[...]
    dw_ref[inner:, :] = (
        lax.dot_general(
            q2_s[...][:, :inner], r, (((0,), (0,)), ((), ())),
            precision=lax.Precision.HIGHEST, preferred_element_type=F32,
        )
        - s_s[...]
    )
    db_ref[...] = jnp.sum(r, axis=0, keepdims=True)


def _split(x):
    high = x.astype(BF16).astype(F32)
    return high, x - high


def _grad_kernel(
    seq_ref, seqk_ref, gain_ref, beta_ref, dq_ref, dk_ref, dw_ref, db_ref,
    out_ref, dqb_ref, dkb_ref,
):
    inner = dqb_ref.shape[1]
    dq = jnp.sum(dq_ref[...], axis=0)[:, :inner]
    dk = jnp.sum(dk_ref[...], axis=0)[:, :inner]
    dq_b, dk_b = dq.astype(BF16), dk.astype(BF16)
    dqb_ref[...] = dq_b
    dkb_ref[...] = dk_b
    b_proj = jnp.concatenate(
        [jnp.sum(dq, axis=0, keepdims=True), jnp.sum(dk, axis=0, keepdims=True)], axis=1
    )
    y_q = (_norm(seq_ref[...])[0] * gain_ref[...] + beta_ref[...]).astype(BF16)
    y_k = (_norm(seqk_ref[...])[0] * gain_ref[...] + beta_ref[...]).astype(BF16)
    dims = (((0,), (0,)), ((), ()))
    w_proj = jnp.concatenate(
        [
            lax.dot_general(y_q, dq_b, dims, preferred_element_type=F32),
            lax.dot_general(y_k, dk_b, dims, preferred_element_type=F32),
        ],
        axis=1,
    )
    n = out_ref.shape[0]
    pair = out_ref.shape[2]
    w_hi, w_lo = _split(dw_ref[...])
    bo_hi, bo_lo = _split(db_ref[...])
    bp_hi, bp_lo = _split(b_proj)
    place = lax.broadcasted_iota(jnp.int32, (n, 8, pair), 1)
    lower = jnp.zeros((n, 8, pair), F32)
    for at, value in enumerate(
        (w_hi[:, None, :], w_lo[:, None, :], bo_hi[None], bo_lo[None], bp_hi[None], bp_lo[None])
    ):
        lower = jnp.where(place == at, jnp.broadcast_to(value, lower.shape), lower)
    out_ref[...] = jnp.concatenate([w_proj.reshape(n, 8, pair), lower], axis=1).astype(BF16)


def _reduce_kernel(x_ref, out_ref, bo_ref, bp_ref):
    total = jnp.sum(x_ref[...].astype(F32), axis=0)
    bo_ref[...] = total[10:11] + total[11:12]
    bp_ref[...] = total[12:13] + total[13:14]
    w_hi, w_lo = _split(total[8:9] + total[9:10])
    tile = jnp.concatenate([total[:8], w_hi, w_lo, jnp.zeros((6, total.shape[1]), F32)], axis=0)
    out_ref[...] = jnp.broadcast_to(tile.astype(BF16)[None], out_ref.shape)


def _unpack_kernel(x_ref, w_proj_ref, w_out_ref):
    x = x_ref[...].astype(F32)
    w_proj_ref[...] = x[:, :8].reshape(w_proj_ref.shape)
    w_out_ref[...] = x[:, 8] + x[:, 9]


def _seq_kernel(seq_ref, gain_ref, w_ref, dq_ref, dk_ref, out_ref):
    normed, inverse = _norm(seq_ref[...])
    dqk = jnp.concatenate([dq_ref[...], dk_ref[...]], axis=1)
    dn = (
        lax.dot_general(dqk, w_ref[...], (((1,), (1,)), ((), ())), preferred_element_type=F32)
        * gain_ref[...]
    )
    out_ref[...] = (
        inverse
        * (
            dn
            - jnp.mean(dn, axis=1, keepdims=True)
            - normed * jnp.mean(dn * normed, axis=1, keepdims=True)
        )
    ).astype(BF16)


def local(n_row, n_col, seq, gain, beta, w_proj, b_proj, w_out, pair_grad):
    shard, width = seq.shape
    pair = w_out.shape[1]
    inner = pair // 2
    rows, cols = pair_grad.shape[:2]
    n = n_row * n_col
    nq, nk = rows // shard, cols // shard
    gain = gain.reshape(1, width)
    beta = beta.reshape(1, width)
    shape = jax.ShapeDtypeStruct

    to_sum = []
    for owner in range(n):
        to_sum.append((owner, (owner % nk) * n_col + owner // nk))
    to_owner = [(b, a) for a, b in to_sum]

    seq_k = lax.ppermute(seq, BOTH, to_sum)
    qk = pl.pallas_call(
        _project_kernel,
        out_shape=shape((n, shard, pair), BF16),
        in_specs=_vmem(5),
        out_specs=pl.BlockSpec(memory_space=pltpu.VMEM),
        compiler_params=_params(32),
    )(seq, gain, beta, w_proj, b_proj.reshape(1, pair))
    qk_all = lax.all_to_all(qk, BOTH, 0, 0, tiled=True)

    dq_part, dk_part, dw_part, db_part = pl.pallas_call(
        _pair_kernel,
        out_shape=(
            shape((nq, shard, pair), F32),
            shape((nk, shard, pair), F32),
            shape((pair, pair), F32),
            shape((1, pair), F32),
        ),
        in_specs=_vmem(2) + [pl.BlockSpec(memory_space=pl.ANY)],
        out_specs=tuple(_vmem(4)),
        scratch_shapes=[
            pltpu.VMEM(pair_grad.shape, BF16),
            pltpu.SemaphoreType.DMA((rows // CHUNK,)),
            pltpu.VMEM((rows, pair), F32),
            pltpu.VMEM((rows // CHUNK, inner, CHUNK), F32),
            pltpu.VMEM((inner + 16, cols), BF16),
            pltpu.VMEM((cols // 2, pair), F32),
            pltpu.VMEM((2 * pair, 2 * pair), BF16),
            pltpu.VMEM((rows, pair), F32),
            pltpu.VMEM((rows, pair), F32),
            pltpu.VMEM((cols // 2, pair), F32),
            pltpu.VMEM((inner, pair), F32),
            pltpu.VMEM((inner, pair), F32),
        ],
        compiler_params=_params(40),
    )(qk_all, w_out, pair_grad)

    dq_in = lax.all_to_all(dq_part, "col", 0, 0, tiled=True)
    dk_in = lax.all_to_all(dk_part, "row", 0, 0, tiled=True)

    slots, dq_b, dk_b = pl.pallas_call(
        _grad_kernel,
        out_shape=(
            shape((n, 16, pair), BF16),
            shape((shard, inner), BF16),
            shape((shard, inner), BF16),
        ),
        in_specs=_vmem(8),
        out_specs=tuple(_vmem(3)),
        compiler_params=_params(40),
    )(seq, seq_k, gain, beta, dq_in, dk_in, dw_part, db_part)
    dk_own = lax.ppermute(dk_b, BOTH, to_owner)
    gathered = lax.all_to_all(slots, BOTH, 0, 0, tiled=True)

    reduced, d_b_out, d_b_proj = pl.pallas_call(
        _reduce_kernel,
        out_shape=(shape((n, 16, pair), BF16), shape((1, pair), F32), shape((1, pair), F32)),
        in_specs=_vmem(1),
        out_specs=tuple(_vmem(3)),
        compiler_params=_params(32),
    )(gathered)
    spread = lax.all_to_all(reduced, BOTH, 0, 0, tiled=True)

    d_seq = pl.pallas_call(
        _seq_kernel,
        out_shape=shape(seq.shape, BF16),
        in_specs=_vmem(5),
        out_specs=pl.BlockSpec(memory_space=pltpu.VMEM),
        compiler_params=_params(32),
    )(seq, gain, w_proj, dq_b, dk_own)

    d_w_proj, d_w_out = pl.pallas_call(
        _unpack_kernel,
        out_shape=(shape((width, pair), F32), shape((pair, pair), F32)),
        in_specs=_vmem(1),
        out_specs=tuple(_vmem(2)),
        compiler_params=_params(32),
    )(spread)
    return d_seq, d_w_proj, d_b_proj.reshape(pair), d_w_out, d_b_out.reshape(pair)


def solution(mesh):
    in_specs = (P(BOTH, None), P(), P(), P(), P(), P(), P("row", "col", None))
    out_specs = (P(BOTH, None), P(), P(), P(), P())
    body = functools.partial(local, mesh.shape["row"], mesh.shape["col"])
    return jax.shard_map(body, mesh=mesh, in_specs=in_specs, out_specs=out_specs, check_vma=False)
```

```python
import functools

import jax
import jax.numpy as jnp
from jax import lax
from jax.experimental import pallas as pl
from jax.experimental.pallas import tpu as pltpu
from jax.sharding import PartitionSpec as P

F32 = jnp.float32
BF16 = jnp.bfloat16
BOTH = ("row", "col")
CHUNK = 48


def _params(mib):
    return pltpu.CompilerParams(vmem_limit_bytes=mib * 2**20)


def _norm(seq):
    source = seq.astype(F32)
    centred = source - jnp.mean(source, axis=1, keepdims=True)
    variance = jnp.mean(centred * centred, axis=1, keepdims=True)
    inverse = 1.0 / jnp.sqrt(variance + 1e-05)
    return centred * inverse, inverse


def _fetch(pairs, sems):
    copies = [pltpu.make_async_copy(a, b, sems.at[n]) for n, (a, b) in enumerate(pairs)]
    for c in copies:
        c.start()
    for c in copies:
        c.wait()


def _project_kernel(
    seq_hbm, gain_hbm, beta_hbm, w_hbm, b_hbm, out_ref, seq_s, gain_s, beta_s, w_s, b_s, sems
):
    _fetch(
        [(seq_hbm, seq_s), (gain_hbm, gain_s), (beta_hbm, beta_s), (w_hbm, w_s), (b_hbm, b_s)],
        sems,
    )
    normed, _ = _norm(seq_s[...])
    y = (normed * gain_s[...] + beta_s[...]).astype(BF16)
    qk = (jnp.dot(y, w_s[...], preferred_element_type=F32) + b_s[...]).astype(BF16)
    out_ref[...] = jnp.broadcast_to(qk[None], out_ref.shape)


def _tile_copies(pg_hbm, pg, sems):
    def copy(ch):
        part = pl.ds(ch * CHUNK, CHUNK)
        return pltpu.make_async_copy(pg_hbm.at[part], pg.at[part], sems.at[ch])

    for ch in range(pg.shape[0] // CHUNK):
        copy(ch).start()
    return copy


def _totals_kernel(pg_hbm, rc_ref, pg, sems):
    rows, cols, pair = pg.shape
    copy = _tile_copies(pg_hbm, pg, sems)
    over_i = pl.ds(rows, cols)
    rc_ref[over_i] = jnp.zeros((cols, pair), F32)

    def chunk(ch, carry):
        copy(ch).wait()
        base = ch * CHUNK
        total = rc_ref[over_i]
        for i in range(CHUNK):
            block = pg[base + i].astype(F32)
            rc_ref[pl.ds(base + i, 1), :] = jnp.sum(block, axis=0, keepdims=True)
            total = total + block
        rc_ref[over_i] = total
        return carry

    lax.fori_loop(0, rows // CHUNK, chunk, 0)


def _own_qk(qk_ref, nq, nk):
    shard, pair = qk_ref.shape[1:]
    inner = pair // 2
    me_r = lax.axis_index("row")
    me_c = lax.axis_index("col")
    q = qk_ref[pl.ds(me_r * nq, nq)].astype(F32).reshape(nq * shard, pair)[:, :inner]
    k = qk_ref[pl.ds(me_c * nk, nk)].astype(F32).reshape(nk * shard, pair)[:, inner:]
    return q, k


def _sums_kernel(
    nq, nk, qk_ref, rc_ref, w_hbm, pg_hbm, out_ref, bp_ref,
    pg, sems, w_s, w_sem, wbd_s, q2_s, k2_s, dq_s, dk_s,
):
    rows, cols, pair = pg.shape
    inner, half = pair // 2, cols // 2
    shard = out_ref.shape[1]
    copy = _tile_copies(pg_hbm, pg, sems)
    _fetch([(w_hbm, w_s)], w_sem)
    q, k = _own_qk(qk_ref, nq, nk)
    q2_s[...] = jnp.concatenate([q, q], axis=1)
    k2_s[...] = jnp.concatenate([k[:half], k[half:]], axis=1)
    wt = w_s[...].astype(F32).T
    blank = jnp.zeros((pair, inner), F32)
    top = jnp.concatenate([wt[:, :inner], blank], axis=1)
    bottom = jnp.concatenate([blank, wt[:, :inner]], axis=1)
    wbd_s[...] = jnp.concatenate([top, bottom], axis=0).astype(BF16)
    gd = jnp.dot(
        rc_ref[...], wt[:, inner:], precision=lax.Precision.HIGHEST, preferred_element_type=F32
    )
    dk_s[...] = jnp.zeros_like(dk_s)
    out_ref[...] = jnp.zeros_like(out_ref)

    def chunk(ch, carry):
        copy(ch).wait()
        base = ch * CHUNK
        dk = dk_s[...]
        k2 = k2_s[...]
        for i in range(CHUNK):
            block = pg[base + i]
            g = jnp.dot(
                jnp.concatenate([block[:half], block[half:]], axis=1),
                wbd_s[...],
                preferred_element_type=F32,
            )
            dq_s[pl.ds(base + i, 1), :] = jnp.sum(g * k2, axis=0, keepdims=True)
            dk = dk + g * q2_s[pl.ds(base + i, 1), :]
        dk_s[...] = dk
        return carry

    lax.fori_loop(0, rows // CHUNK, chunk, 0)
    dq = dq_s[...]
    dq = dq[:, :inner] + dq[:, inner:] + gd[:rows]
    dk = dk_s[...]
    dk = jnp.concatenate([dk[:, :inner], dk[:, inner:]], axis=0) - gd[rows:]
    bp_ref[...] = jnp.concatenate(
        [jnp.sum(dq, axis=0, keepdims=True), jnp.sum(dk, axis=0, keepdims=True)], axis=1
    )
    dq = jnp.concatenate([dq, jnp.zeros_like(dq)], axis=1).reshape(nq, shard, pair)
    dk = jnp.concatenate([jnp.zeros_like(dk), dk], axis=1).reshape(nk, shard, pair)
    at_q = pl.ds(lax.axis_index("row") * nq, nq)
    at_k = pl.ds(lax.axis_index("col") * nk, nk)
    out_ref[at_q] = dq.astype(BF16)
    out_ref[at_k] = (out_ref[at_k].astype(F32) + dk).astype(BF16)


def _weight_kernel(
    nq, nk, qk_ref, rc_ref, pg_hbm, dw_ref, db_ref, pg, sems, qt_s, kt_s, dwp_s
):
    rows, cols, pair = pg.shape
    inner = pair // 2
    n_chunks = rows // CHUNK
    copy = _tile_copies(pg_hbm, pg, sems)
    q, k = _own_qk(qk_ref, nq, nk)
    qt, kt = q.T, k.T
    for ch in range(n_chunks):
        qt_s[ch] = qt[:, ch * CHUNK : (ch + 1) * CHUNK]
    kt_s[...] = kt.astype(BF16)
    dwp_s[...] = jnp.zeros_like(dwp_s)
    rc = rc_ref[...]
    dw_ref[inner:, :] = jnp.dot(
        jnp.concatenate([qt, -kt], axis=1),
        rc,
        precision=lax.Precision.HIGHEST,
        preferred_element_type=F32,
    )
    db_ref[...] = jnp.sum(rc[:rows], axis=0, keepdims=True)

    def chunk(ch, carry):
        copy(ch).wait()
        base = ch * CHUNK
        dwp = dwp_s[...]
        for i in range(0, CHUNK, 2):
            a = jnp.dot(
                kt_s[...],
                jnp.concatenate([pg[base + i], pg[base + i + 1]], axis=1),
                preferred_element_type=F32,
            )
            dwp = dwp + (
                a[:, :pair] * qt_s[ch, :, i : i + 1] + a[:, pair:] * qt_s[ch, :, i + 1 : i + 2]
            )
        dwp_s[...] = dwp
        return carry

    lax.fori_loop(0, n_chunks, chunk, 0)
    dw_ref[:inner, :] = dwp_s[...]


def _split(x):
    high = x.astype(BF16).astype(F32)
    return high, x - high


def _grad_kernel(
    seq_ref, gain_ref, beta_ref, dqk_ref, dw_ref, db_ref, bp_ref, out_ref, dqkb_ref
):
    dqk_b = jnp.sum(dqk_ref[...].astype(F32), axis=0).astype(BF16)
    dqkb_ref[...] = dqk_b
    y = (_norm(seq_ref[...])[0] * gain_ref[...] + beta_ref[...]).astype(BF16)
    w_proj = lax.dot_general(y, dqk_b, (((0,), (0,)), ((), ())), preferred_element_type=F32)
    n = out_ref.shape[0]
    pair = out_ref.shape[2]
    w_hi, w_lo = _split(dw_ref[...])
    bo_hi, bo_lo = _split(db_ref[...])
    bp_hi, bp_lo = _split(bp_ref[...])
    place = lax.broadcasted_iota(jnp.int32, (n, 8, pair), 1)
    lower = jnp.zeros((n, 8, pair), F32)
    for at, value in enumerate(
        (w_hi[:, None, :], w_lo[:, None, :], bo_hi[None], bo_lo[None], bp_hi[None], bp_lo[None])
    ):
        lower = jnp.where(place == at, jnp.broadcast_to(value, lower.shape), lower)
    out_ref[...] = jnp.concatenate([w_proj.reshape(n, 8, pair), lower], axis=1).astype(BF16)


def _reduce_kernel(x_ref, out_ref, bo_ref, bp_ref):
    total = jnp.sum(x_ref[...].astype(F32), axis=0)
    bo_ref[...] = total[10:11] + total[11:12]
    bp_ref[...] = total[12:13] + total[13:14]
    w_hi, w_lo = _split(total[8:9] + total[9:10])
    tile = jnp.concatenate([total[:8], w_hi, w_lo, jnp.zeros((6, total.shape[1]), F32)], axis=0)
    out_ref[...] = jnp.broadcast_to(tile.astype(BF16)[None], out_ref.shape)


def _unpack_kernel(x_ref, w_proj_ref, w_out_ref):
    x = x_ref[...].astype(F32)
    w_proj_ref[...] = x[:, :8].reshape(w_proj_ref.shape)
    w_out_ref[...] = x[:, 8] + x[:, 9]


def _seq_kernel(seq_ref, gain_ref, w_ref, dqk_ref, out_ref):
    normed, inverse = _norm(seq_ref[...])
    dqk = dqk_ref[...]
    dn = (
        lax.dot_general(dqk, w_ref[...], (((1,), (1,)), ((), ())), preferred_element_type=F32)
        * gain_ref[...]
    )
    out_ref[...] = (
        inverse
        * (
            dn
            - jnp.mean(dn, axis=1, keepdims=True)
            - normed * jnp.mean(dn * normed, axis=1, keepdims=True)
        )
    ).astype(BF16)


def local(n_row, n_col, seq, gain, beta, w_proj, b_proj, w_out, pair_grad):
    shard, width = seq.shape
    pair = w_out.shape[1]
    inner = pair // 2
    rows, cols = pair_grad.shape[:2]
    n = n_row * n_col
    nq, nk = rows // shard, cols // shard
    gain = gain.reshape(1, width)
    beta = beta.reshape(1, width)
    shape = jax.ShapeDtypeStruct

    vmem = pl.BlockSpec(memory_space=pltpu.VMEM)
    hbm = pl.BlockSpec(memory_space=pltpu.HBM)
    tile = [pltpu.VMEM(pair_grad.shape, BF16), pltpu.SemaphoreType.DMA((rows // CHUNK,))]

    qk = pl.pallas_call(
        _project_kernel,
        out_shape=shape((n, shard, pair), BF16),
        in_specs=[hbm] * 5,
        out_specs=vmem,
        scratch_shapes=[
            pltpu.VMEM((shard, width), BF16),
            pltpu.VMEM((1, width), F32),
            pltpu.VMEM((1, width), F32),
            pltpu.VMEM((width, pair), BF16),
            pltpu.VMEM((1, pair), F32),
            pltpu.SemaphoreType.DMA((5,)),
        ],
        compiler_params=_params(60),
    )(seq, gain, beta, w_proj, b_proj.reshape(1, pair))
    qk_all = lax.all_to_all(qk, BOTH, 0, 0, tiled=True)

    rc = pl.pallas_call(
        _totals_kernel,
        out_shape=shape((rows + cols, pair), F32),
        in_specs=[hbm],
        out_specs=vmem,
        scratch_shapes=tile,
        compiler_params=_params(60),
        cost_estimate=pl.CostEstimate(
            flops=4 * rows * cols * pair * pair, bytes_accessed=3 * rows * cols * pair, transcendentals=0
        ),
    )(pair_grad)

    dqk_part, bp_part = pl.pallas_call(
        functools.partial(_sums_kernel, nq, nk),
        out_shape=(shape((n, shard, pair), BF16), shape((1, pair), F32)),
        in_specs=[vmem, vmem, hbm, hbm],
        out_specs=(vmem,) * 2,
        scratch_shapes=tile
        + [
            pltpu.VMEM((pair, pair), BF16),
            pltpu.SemaphoreType.DMA((1,)),
            pltpu.VMEM((2 * pair, pair), BF16),
            pltpu.VMEM((rows, pair), F32),
            pltpu.VMEM((cols // 2, pair), F32),
            pltpu.VMEM((rows, pair), F32),
            pltpu.VMEM((cols // 2, pair), F32),
        ],
        compiler_params=_params(40),
    )(qk_all, rc, w_out, pair_grad)
    dqk_in = lax.all_to_all(dqk_part, BOTH, 0, 0, tiled=True)

    dw_part, db_part = pl.pallas_call(
        functools.partial(_weight_kernel, nq, nk),
        out_shape=(shape((pair, pair), F32), shape((1, pair), F32)),
        in_specs=[vmem, vmem, hbm],
        out_specs=(vmem,) * 2,
        scratch_shapes=tile
        + [
            pltpu.VMEM((rows // CHUNK, inner, CHUNK), F32),
            pltpu.VMEM((inner, cols), BF16),
            pltpu.VMEM((inner, pair), F32),
        ],
        compiler_params=_params(40),
        cost_estimate=pl.CostEstimate(
            flops=4 * rows * cols * pair * pair, bytes_accessed=2 * rows * cols * pair, transcendentals=0
        ),
    )(qk_all, rc, pair_grad)

    slots, dqk_b = pl.pallas_call(
        _grad_kernel,
        out_shape=(shape((n, 16, pair), BF16), shape((shard, pair), BF16)),
        in_specs=[vmem] * 7,
        out_specs=(vmem,) * 2,
        compiler_params=_params(32),
    )(seq, gain, beta, dqk_in, dw_part, db_part, bp_part)
    gathered = lax.all_to_all(slots, BOTH, 0, 0, tiled=True)

    reduced, d_b_out, d_b_proj = pl.pallas_call(
        _reduce_kernel,
        out_shape=(shape((n, 16, pair), BF16), shape((1, pair), F32), shape((1, pair), F32)),
        in_specs=[vmem],
        out_specs=(vmem,) * 3,
        compiler_params=_params(32),
    )(gathered)
    spread = lax.all_to_all(reduced, BOTH, 0, 0, tiled=True)

    d_seq = pl.pallas_call(
        _seq_kernel,
        out_shape=shape(seq.shape, BF16),
        in_specs=[vmem] * 4,
        out_specs=vmem,
        compiler_params=_params(32),
    )(seq, gain, w_proj, dqk_b)

    d_w_proj, d_w_out = pl.pallas_call(
        _unpack_kernel,
        out_shape=(shape((width, pair), F32), shape((pair, pair), F32)),
        in_specs=[vmem],
        out_specs=(vmem,) * 2,
        compiler_params=_params(32),
    )(spread)
    return d_seq, d_w_proj, d_b_proj.reshape(pair), d_w_out, d_b_out.reshape(pair)


def solution(mesh):
    in_specs = (P(BOTH, None), P(), P(), P(), P(), P(), P("row", "col", None))
    out_specs = (P(BOTH, None), P(), P(), P(), P())
    body = functools.partial(local, mesh.shape["row"], mesh.shape["col"])
    return jax.shard_map(body, mesh=mesh, in_specs=in_specs, out_specs=out_specs, check_vma=False)
```

```python
import functools

import jax
import jax.numpy as jnp
from jax import lax
from jax.experimental import pallas as pl
from jax.experimental.pallas import tpu as pltpu
from jax.sharding import PartitionSpec as P

F32 = jnp.float32
BF16 = jnp.bfloat16
BOTH = ("row", "col")
CHUNK = 48


def _params(mib):
    return pltpu.CompilerParams(vmem_limit_bytes=mib * 2**20)


def _norm(seq):
    source = seq.astype(F32)
    centred = source - jnp.mean(source, axis=1, keepdims=True)
    variance = jnp.mean(centred * centred, axis=1, keepdims=True)
    inverse = 1.0 / jnp.sqrt(variance + 1e-05)
    return centred * inverse, inverse


def _fetch(pairs, sems):
    copies = [pltpu.make_async_copy(a, b, sems.at[n]) for n, (a, b) in enumerate(pairs)]
    for c in copies:
        c.start()
    for c in copies:
        c.wait()


def _project_kernel(
    seq_hbm, gain_hbm, beta_hbm, w_hbm, b_hbm, out_ref, seq_s, gain_s, beta_s, w_s, b_s, sems
):
    _fetch(
        [(seq_hbm, seq_s), (gain_hbm, gain_s), (beta_hbm, beta_s), (w_hbm, w_s), (b_hbm, b_s)],
        sems,
    )
    normed, _ = _norm(seq_s[...])
    y = (normed * gain_s[...] + beta_s[...]).astype(BF16)
    qk = (jnp.dot(y, w_s[...], preferred_element_type=F32) + b_s[...]).astype(BF16)
    out_ref[...] = jnp.broadcast_to(qk[None], out_ref.shape)


def _tile_copies(pg_hbm, pg, sems):
    def copy(ch):
        part = pl.ds(ch * CHUNK, CHUNK)
        return pltpu.make_async_copy(pg_hbm.at[part], pg.at[part], sems.at[ch])

    for ch in range(pg.shape[0] // CHUNK):
        copy(ch).start()
    return copy


def _totals_kernel(pg_hbm, rc_hbm, pg, sems, rc_ref, rc_sem):
    rows, cols, pair = pg.shape
    copy = _tile_copies(pg_hbm, pg, sems)
    over_i = pl.ds(rows, cols)
    rc_ref[over_i] = jnp.zeros((cols, pair), F32)

    def chunk(ch, carry):
        copy(ch).wait()
        base = ch * CHUNK
        total = rc_ref[over_i]
        for i in range(CHUNK):
            block = pg[base + i].astype(F32)
            rc_ref[pl.ds(base + i, 1), :] = jnp.sum(block, axis=0, keepdims=True)
            total = total + block
        rc_ref[over_i] = total
        return carry

    lax.fori_loop(0, rows // CHUNK, chunk, 0)
    _fetch([(rc_ref, rc_hbm)], rc_sem)


def _pack(x):
    n, shard, inner = x.shape
    x = x.reshape(n, shard // 8, 8, inner)
    return jnp.concatenate([x[:, :, :4], x[:, :, 4:]], axis=3)


def _unpack(x):
    inner = x.shape[-1] // 2
    x = jnp.concatenate([x[:, :, :inner], x[:, :, inner:]], axis=1)
    return x.reshape(x.shape[0] * 8, inner)


def _own_slots(qk_hbm, q_s, k_s):
    nq, nk = q_s.shape[0], k_s.shape[0]
    return [
        (qk_hbm.at[pl.ds(lax.axis_index("row") * nq, nq)], q_s),
        (qk_hbm.at[pl.ds(lax.axis_index("col") * nk, nk)], k_s),
    ]


def _own_qk(q_s, k_s):
    nq, shard, pair = q_s.shape
    inner = pair // 2
    q = q_s[...].astype(F32).reshape(nq * shard, pair)[:, :inner]
    k = k_s[...].astype(F32).reshape(k_s.shape[0] * shard, pair)[:, inner:]
    return q, k


def _sums_kernel(
    nq, nk, qk_hbm, rc_hbm, w_hbm, pg_hbm, seqk_hbm, out_ref, home_ref, bp_ref,
    pg, sems, q_s, k_s, w_s, rc_s, in_sems, wbd_s, q2_s, k2_s, dq_s, dk_s, piece_s,
):
    rows, cols, pair = pg.shape
    inner, half = pair // 2, cols // 2
    shard = home_ref.shape[0]
    copy = _tile_copies(pg_hbm, pg, sems)
    del seqk_hbm
    _fetch(_own_slots(qk_hbm, q_s, k_s) + [(w_hbm, w_s), (rc_hbm, rc_s)], in_sems)
    q, k = _own_qk(q_s, k_s)
    q2_s[...] = jnp.concatenate([q, q], axis=1)
    k2_s[...] = jnp.concatenate([k[:half], k[half:]], axis=1)
    wt = w_s[...].astype(F32).T
    blank = jnp.zeros((pair, inner), F32)
    top = jnp.concatenate([wt[:, :inner], blank], axis=1)
    bottom = jnp.concatenate([blank, wt[:, :inner]], axis=1)
    wbd_s[...] = jnp.concatenate([top, bottom], axis=0).astype(BF16)
    gd = jnp.dot(
        rc_s[...], wt[:, inner:], precision=lax.Precision.HIGHEST, preferred_element_type=F32
    )
    dk_s[...] = jnp.zeros_like(dk_s)
    out_ref[...] = jnp.zeros_like(out_ref)

    def chunk(ch, carry):
        copy(ch).wait()
        base = ch * CHUNK
        dk = dk_s[...]
        k2 = k2_s[...]
        for i in range(CHUNK):
            block = pg[base + i]
            g = jnp.dot(
                jnp.concatenate([block[:half], block[half:]], axis=1),
                wbd_s[...],
                preferred_element_type=F32,
            )
            dq_s[pl.ds(base + i, 1), :] = jnp.sum(g * k2, axis=0, keepdims=True)
            dk = dk + g * q2_s[pl.ds(base + i, 1), :]
        dk_s[...] = dk
        return carry

    lax.fori_loop(0, rows // CHUNK, chunk, 0)
    dq = dq_s[...]
    dq = dq[:, :inner] + dq[:, inner:] + gd[:rows]
    dk = dk_s[...]
    dk = jnp.concatenate([dk[:, :inner], dk[:, inner:]], axis=0) - gd[rows:]
    bp_ref[...] = jnp.concatenate(
        [jnp.sum(dq, axis=0, keepdims=True), jnp.sum(dk, axis=0, keepdims=True)], axis=1
    )
    me_r = lax.axis_index("row")
    me_c = lax.axis_index("col")
    dk = dk.reshape(nk, shard, inner)
    piece_s[...] = dk
    home_ref[...] = piece_s[me_r]
    packed = _pack(dk).astype(BF16)
    for m in range(nk):
        out_ref[m * nq + me_c] = packed[m]
    out_ref[pl.ds(me_r * nq, nq)] = _pack(dq.reshape(nq, shard, inner)).astype(BF16)


def _weight_kernel(
    qk_hbm, rc_hbm, pg_hbm, dw_ref, db_ref, pg, sems, q_s, k_s, rc_s, in_sems, qt_s, kt_s, dwp_s
):
    rows, cols, pair = pg.shape
    inner = pair // 2
    n_chunks = rows // CHUNK
    copy = _tile_copies(pg_hbm, pg, sems)
    _fetch(_own_slots(qk_hbm, q_s, k_s) + [(rc_hbm, rc_s)], in_sems)
    q, k = _own_qk(q_s, k_s)
    qt, kt = q.T, k.T
    for ch in range(n_chunks):
        qt_s[ch] = qt[:, ch * CHUNK : (ch + 1) * CHUNK]
    kt_s[...] = kt.astype(BF16)
    dwp_s[...] = jnp.zeros_like(dwp_s)
    rc = rc_s[...]
    dw_ref[inner:, :] = jnp.dot(
        jnp.concatenate([qt, -kt], axis=1),
        rc,
        precision=lax.Precision.HIGHEST,
        preferred_element_type=F32,
    )
    db_ref[...] = jnp.sum(rc[:rows], axis=0, keepdims=True)

    def chunk(ch, carry):
        copy(ch).wait()
        base = ch * CHUNK
        dwp = dwp_s[...]
        for i in range(0, CHUNK, 2):
            a = jnp.dot(
                kt_s[...],
                jnp.concatenate([pg[base + i], pg[base + i + 1]], axis=1),
                preferred_element_type=F32,
            )
            dwp = dwp + (
                a[:, :pair] * qt_s[ch, :, i : i + 1] + a[:, pair:] * qt_s[ch, :, i + 1 : i + 2]
            )
        dwp_s[...] = dwp
        return carry

    lax.fori_loop(0, n_chunks, chunk, 0)
    dw_ref[:inner, :] = dwp_s[...]


def _split(x):
    high = x.astype(BF16).astype(F32)
    return high, x - high


def _grad_kernel(
    nq, nk, seq_ref, seqk_ref, gain_ref, beta_ref, dqk_ref, home_ref, dw_ref, db_ref, bp_ref,
    out_ref, dqb_ref, dkb_ref,
):
    me_r = lax.axis_index("row")
    me_c = lax.axis_index("col")
    dq = _unpack(jnp.sum(dqk_ref[pl.ds(me_r * nq, nq)].astype(F32), axis=0))
    dk = home_ref[...]
    for m in range(nk):
        part = _unpack(dqk_ref[m * nq + me_c].astype(F32))
        dk = dk + jnp.where(me_r == m, jnp.zeros_like(part), part)
    dq_b, dk_b = dq.astype(BF16), dk.astype(BF16)
    dqb_ref[...] = dq_b
    dkb_ref[...] = dk_b
    dims = (((0,), (0,)), ((), ()))

    def rows_of(ref, cotangent):
        y = (_norm(ref[...])[0] * gain_ref[...] + beta_ref[...]).astype(BF16)
        return lax.dot_general(y, cotangent, dims, preferred_element_type=F32)

    w_proj = jnp.concatenate([rows_of(seq_ref, dq_b), rows_of(seqk_ref, dk_b)], axis=1)
    n, _, quarter, pair = out_ref.shape
    w_proj = w_proj.reshape(n, 2 * quarter, pair)
    out_ref[:, 0] = w_proj[:, :quarter].astype(BF16)
    out_ref[:, 1] = w_proj[:, quarter:].astype(BF16)
    bp_hi, bp_lo = _split(bp_ref[...])
    place = lax.broadcasted_iota(jnp.int32, (n, quarter, pair), 1)
    last = jnp.broadcast_to(dw_ref[...][:, None, :], place.shape)
    for at, value in enumerate((db_ref[...], bp_hi, bp_lo), 1):
        last = jnp.where(place == at, jnp.broadcast_to(value[None], place.shape), last)
    out_ref[:, 2] = last.astype(BF16)


def _reduce_kernel(x_ref, out_ref, bo_ref, bp_ref):
    total = jnp.sum(x_ref[...].astype(F32), axis=0)
    last = total[2]
    bo_ref[...] = last[1:2]
    bp_ref[...] = last[2:3] + last[3:4]
    w_hi, w_lo = _split(last[0:1])
    last = jnp.concatenate([w_hi, w_lo, jnp.zeros((2, last.shape[1]), F32)], axis=0)
    tile = jnp.concatenate([total[:2], last[None]], axis=0).astype(BF16)
    out_ref[...] = jnp.broadcast_to(tile[None], out_ref.shape)


def _unpack_kernel(x_ref, w_proj_ref, w_out_ref):
    x = x_ref[...].astype(F32)
    w_proj_ref[...] = jnp.concatenate([x[:, 0], x[:, 1]], axis=1).reshape(w_proj_ref.shape)
    w_out_ref[...] = x[:, 2, 0] + x[:, 2, 1]


def _seq_kernel(seq_ref, gain_ref, w_ref, dq_ref, dk_ref, out_ref):
    normed, inverse = _norm(seq_ref[...])
    dqk = jnp.concatenate([dq_ref[...], dk_ref[...]], axis=1)
    dn = (
        lax.dot_general(dqk, w_ref[...], (((1,), (1,)), ((), ())), preferred_element_type=F32)
        * gain_ref[...]
    )
    out_ref[...] = (
        inverse
        * (
            dn
            - jnp.mean(dn, axis=1, keepdims=True)
            - normed * jnp.mean(dn * normed, axis=1, keepdims=True)
        )
    ).astype(BF16)


def local(n_row, n_col, seq, gain, beta, w_proj, b_proj, w_out, pair_grad):
    shard, width = seq.shape
    pair = w_out.shape[1]
    inner = pair // 2
    rows, cols = pair_grad.shape[:2]
    n = n_row * n_col
    nq, nk = rows // shard, cols // shard
    gain = gain.reshape(1, width)
    beta = beta.reshape(1, width)
    shape = jax.ShapeDtypeStruct

    vmem = pl.BlockSpec(memory_space=pltpu.VMEM)
    hbm = pl.BlockSpec(memory_space=pltpu.HBM)
    tile = [pltpu.VMEM(pair_grad.shape, BF16), pltpu.SemaphoreType.DMA((rows // CHUNK,))]

    qk = pl.pallas_call(
        _project_kernel,
        out_shape=shape((n, shard, pair), BF16),
        in_specs=[hbm] * 5,
        out_specs=vmem,
        scratch_shapes=[
            pltpu.VMEM((shard, width), BF16),
            pltpu.VMEM((1, width), F32),
            pltpu.VMEM((1, width), F32),
            pltpu.VMEM((width, pair), BF16),
            pltpu.VMEM((1, pair), F32),
            pltpu.SemaphoreType.DMA((5,)),
        ],
        compiler_params=_params(60),
    )(seq, gain, beta, w_proj, b_proj.reshape(1, pair))
    to_sum = [(d, (d % nk) * n_col + d // nk) for d in range(n)]
    to_owner = [(b, a) for a, b in to_sum]
    seq_k = lax.ppermute(seq, BOTH, to_sum)
    qk_all = lax.all_to_all(qk, BOTH, 0, 0, tiled=True)

    rc = pl.pallas_call(
        _totals_kernel,
        out_shape=shape((rows + cols, pair), F32),
        in_specs=[hbm],
        out_specs=hbm,
        scratch_shapes=tile + [pltpu.VMEM((rows + cols, pair), F32), pltpu.SemaphoreType.DMA((1,))],
        compiler_params=_params(60),
        cost_estimate=pl.CostEstimate(
            flops=4 * rows * cols * pair * pair, bytes_accessed=3 * rows * cols * pair, transcendentals=0
        ),
    )(pair_grad)

    own = [pltpu.VMEM((nq, shard, pair), BF16), pltpu.VMEM((nk, shard, pair), BF16)]
    slot = shape((n, shard // 8, 4, pair), BF16)
    dqk_part, home, bp_part = pl.pallas_call(
        functools.partial(_sums_kernel, nq, nk),
        out_shape=(slot, shape((shard, inner), F32), shape((1, pair), F32)),
        in_specs=[hbm] * 5,
        out_specs=(vmem,) * 3,
        scratch_shapes=tile
        + own
        + [
            pltpu.VMEM((pair, pair), BF16),
            pltpu.VMEM((rows + cols, pair), F32),
            pltpu.SemaphoreType.DMA((4,)),
            pltpu.VMEM((2 * pair, pair), BF16),
            pltpu.VMEM((rows, pair), F32),
            pltpu.VMEM((cols // 2, pair), F32),
            pltpu.VMEM((rows, pair), F32),
            pltpu.VMEM((cols // 2, pair), F32),
            pltpu.VMEM((nk, shard, inner), F32),
        ],
        compiler_params=_params(40),
    )(qk_all, rc, w_out, pair_grad, seq_k)
    dqk_in = lax.all_to_all(dqk_part, BOTH, 0, 0, tiled=True)

    dw_part, db_part = pl.pallas_call(
        _weight_kernel,
        out_shape=(shape((pair, pair), F32), shape((1, pair), F32)),
        in_specs=[hbm] * 3,
        out_specs=(vmem,) * 2,
        scratch_shapes=tile
        + own
        + [
            pltpu.VMEM((rows + cols, pair), F32),
            pltpu.SemaphoreType.DMA((3,)),
            pltpu.VMEM((rows // CHUNK, inner, CHUNK), F32),
            pltpu.VMEM((inner, cols), BF16),
            pltpu.VMEM((inner, pair), F32),
        ],
        compiler_params=_params(40),
        cost_estimate=pl.CostEstimate(
            flops=4 * rows * cols * pair * pair, bytes_accessed=2 * rows * cols * pair, transcendentals=0
        ),
    )(qk_all, rc, pair_grad)

    slots, dq_b, dk_b = pl.pallas_call(
        functools.partial(_grad_kernel, nq, nk),
        out_shape=(slot, shape((shard, inner), BF16), shape((shard, inner), BF16)),
        in_specs=[vmem] * 9,
        out_specs=(vmem,) * 3,
        compiler_params=_params(32),
    )(seq, seq_k, gain, beta, dqk_in, home, dw_part, db_part, bp_part)
    gathered = lax.all_to_all(slots, BOTH, 0, 0, tiled=True)
    dk_own = lax.ppermute(dk_b, BOTH, to_owner)

    reduced, d_b_out, d_b_proj = pl.pallas_call(
        _reduce_kernel,
        out_shape=(slot, shape((1, pair), F32), shape((1, pair), F32)),
        in_specs=[vmem],
        out_specs=(vmem,) * 3,
        compiler_params=_params(32),
    )(gathered)
    spread = lax.all_to_all(reduced, BOTH, 0, 0, tiled=True)

    d_seq = pl.pallas_call(
        _seq_kernel,
        out_shape=shape(seq.shape, BF16),
        in_specs=[vmem] * 5,
        out_specs=vmem,
        compiler_params=_params(32),
    )(seq, gain, w_proj, dq_b, dk_own)

    d_w_proj, d_w_out = pl.pallas_call(
        _unpack_kernel,
        out_shape=(shape((width, pair), F32), shape((pair, pair), F32)),
        in_specs=[vmem],
        out_specs=(vmem,) * 2,
        compiler_params=_params(32),
    )(spread)
    return d_seq, d_w_proj, d_b_proj.reshape(pair), d_w_out, d_b_out.reshape(pair)


def solution(mesh):
    in_specs = (P(BOTH, None), P(), P(), P(), P(), P(), P("row", "col", None))
    out_specs = (P(BOTH, None), P(), P(), P(), P())
    body = functools.partial(local, mesh.shape["row"], mesh.shape["col"])
    return jax.shard_map(body, mesh=mesh, in_specs=in_specs, out_specs=out_specs, check_vma=False)
```

```python
import functools

import jax
import jax.numpy as jnp
from jax import lax
from jax.experimental import pallas as pl
from jax.experimental.pallas import tpu as pltpu
from jax.sharding import PartitionSpec as P

F32 = jnp.float32
BF16 = jnp.bfloat16
BOTH = ("row", "col")
CHUNK = 64


def _params(mib):
    return pltpu.CompilerParams(vmem_limit_bytes=mib * 2**20)


def _norm(seq):
    source = seq.astype(F32)
    centred = source - jnp.mean(source, axis=1, keepdims=True)
    variance = jnp.mean(centred * centred, axis=1, keepdims=True)
    inverse = 1.0 / jnp.sqrt(variance + 1e-05)
    return centred * inverse, inverse


def _start(pairs, sems):
    copies = [pltpu.make_async_copy(a, b, sems.at[n]) for n, (a, b) in enumerate(pairs)]
    for c in copies:
        c.start()
    return copies


def _fetch(pairs, sems):
    for c in _start(pairs, sems):
        c.wait()


def _spread(block_s, out_hbm, sems):
    count = block_s.shape[0]
    parts = range(0, out_hbm.shape[0], count)
    _fetch([(block_s, out_hbm.at[pl.ds(at, count)]) for at in parts], sems)


def _project_kernel(
    seq_hbm, gain_hbm, beta_hbm, w_hbm, b_hbm, out_hbm,
    seq_s, gain_s, beta_s, w_s, b_s, sems, block_s, out_sems,
):
    copies = _start(
        [(seq_hbm, seq_s), (gain_hbm, gain_s), (beta_hbm, beta_s), (w_hbm, w_s), (b_hbm, b_s)],
        sems,
    )
    copies[0].wait()
    normed, _ = _norm(seq_s[...])
    for c in copies[1:]:
        c.wait()
    y = (normed * gain_s[...] + beta_s[...]).astype(BF16)
    qk = (jnp.dot(y, w_s[...], preferred_element_type=F32) + b_s[...]).astype(BF16)
    block_s[...] = jnp.broadcast_to(qk[None], block_s.shape)
    _spread(block_s, out_hbm, out_sems)


def _tile_copies(pg_hbm, pg, sems):
    def copy(ch):
        part = pl.ds(ch * CHUNK, CHUNK)
        return pltpu.make_async_copy(pg_hbm.at[part], pg.at[part], sems.at[ch])

    for ch in range(pg.shape[0] // CHUNK):
        copy(ch).start()
    return copy


def _totals_kernel(pg_hbm, rc_hbm, pg, sems, rc_ref, rc_sem):
    rows, cols, pair = pg.shape
    copy = _tile_copies(pg_hbm, pg, sems)
    over_i = pl.ds(rows, cols)
    rc_ref[over_i] = jnp.zeros((cols, pair), F32)

    def chunk(ch, carry):
        copy(ch).wait()
        base = ch * CHUNK
        total = rc_ref[over_i]
        for i in range(CHUNK):
            block = pg[base + i].astype(F32)
            rc_ref[pl.ds(base + i, 1), :] = jnp.sum(block, axis=0, keepdims=True)
            total = total + block
        rc_ref[over_i] = total
        return carry

    lax.fori_loop(0, rows // CHUNK, chunk, 0)
    _fetch([(rc_ref, rc_hbm)], rc_sem)


def _pack(x):
    n, shard, inner = x.shape
    x = x.reshape(n, shard // 8, 8, inner)
    return jnp.concatenate([x[:, :, :4], x[:, :, 4:]], axis=3)


def _unpack(x):
    inner = x.shape[-1] // 2
    x = jnp.concatenate([x[:, :, :inner], x[:, :, inner:]], axis=1)
    return x.reshape(x.shape[0] * 8, inner)


def _own_slots(qk_hbm, q_s, k_s):
    nq, nk = q_s.shape[0], k_s.shape[0]
    return [
        (qk_hbm.at[pl.ds(lax.axis_index("row") * nq, nq)], q_s),
        (qk_hbm.at[pl.ds(lax.axis_index("col") * nk, nk)], k_s),
    ]


def _own_qk(q_s, k_s):
    nq, shard, pair = q_s.shape
    inner = pair // 2
    q = q_s[...].astype(F32).reshape(nq * shard, pair)[:, :inner]
    k = k_s[...].astype(F32).reshape(k_s.shape[0] * shard, pair)[:, inner:]
    return q, k


def _sums_kernel(
    nq, nk, qk_hbm, rc_hbm, w_hbm, pg_hbm, seqk_hbm, out_ref, home_ref, bp_ref,
    pg, sems, q_s, k_s, w_s, rc_s, in_sems, wbd_s, q2_s, k2_s, dq_s, dk_s, piece_s,
):
    rows, cols, pair = pg.shape
    inner, half = pair // 2, cols // 2
    shard = home_ref.shape[0]
    del seqk_hbm
    small = _start(_own_slots(qk_hbm, q_s, k_s) + [(w_hbm, w_s), (rc_hbm, rc_s)], in_sems)
    copy = _tile_copies(pg_hbm, pg, sems)
    for c in small[:3]:
        c.wait()
    q, k = _own_qk(q_s, k_s)
    q2_s[...] = jnp.concatenate([q, q], axis=1)
    k2_s[...] = jnp.concatenate([k[:half], k[half:]], axis=1)
    wt = w_s[...].astype(F32).T
    blank = jnp.zeros((pair, inner), F32)
    top = jnp.concatenate([wt[:, :inner], blank], axis=1)
    bottom = jnp.concatenate([blank, wt[:, :inner]], axis=1)
    wbd_s[...] = jnp.concatenate([top, bottom], axis=0).astype(BF16)
    dk_s[...] = jnp.zeros_like(dk_s)
    out_ref[...] = jnp.zeros_like(out_ref)

    def chunk(ch, carry):
        copy(ch).wait()
        base = ch * CHUNK
        dk = dk_s[...]
        k2 = k2_s[...]
        for i in range(CHUNK):
            block = pg[base + i]
            g = jnp.dot(
                jnp.concatenate([block[:half], block[half:]], axis=1),
                wbd_s[...],
                preferred_element_type=F32,
            )
            dq_s[pl.ds(base + i, 1), :] = jnp.sum(g * k2, axis=0, keepdims=True)
            dk = dk + g * q2_s[pl.ds(base + i, 1), :]
        dk_s[...] = dk
        return carry

    lax.fori_loop(0, rows // CHUNK, chunk, 0)
    small[3].wait()
    gd = jnp.dot(
        rc_s[...], w_s[...].astype(F32).T[:, inner:], precision=lax.Precision.HIGHEST, preferred_element_type=F32
    )
    dq = dq_s[...]
    dq = dq[:, :inner] + dq[:, inner:] + gd[:rows]
    dk = dk_s[...]
    dk = jnp.concatenate([dk[:, :inner], dk[:, inner:]], axis=0) - gd[rows:]
    bp_ref[...] = jnp.concatenate(
        [jnp.sum(dq, axis=0, keepdims=True), jnp.sum(dk, axis=0, keepdims=True)], axis=1
    )
    me_r = lax.axis_index("row")
    me_c = lax.axis_index("col")
    dk = dk.reshape(nk, shard, inner)
    piece_s[...] = dk
    home_ref[...] = piece_s[me_r]
    packed = _pack(dk).astype(BF16)
    for m in range(nk):
        out_ref[m * nq + me_c] = packed[m]
    out_ref[pl.ds(me_r * nq, nq)] = _pack(dq.reshape(nq, shard, inner)).astype(BF16)


def _weight_kernel(
    qk_hbm, rc_hbm, pg_hbm, dw_ref, db_ref, pg, sems, q_s, k_s, rc_s, in_sems, qt_s, kt_s, dwp_s
):
    rows, cols, pair = pg.shape
    inner = pair // 2
    n_chunks = rows // CHUNK
    copy = _tile_copies(pg_hbm, pg, sems)
    _fetch(_own_slots(qk_hbm, q_s, k_s) + [(rc_hbm, rc_s)], in_sems)
    q, k = _own_qk(q_s, k_s)
    qt, kt = q.T, k.T
    for ch in range(n_chunks):
        qt_s[ch] = qt[:, ch * CHUNK : (ch + 1) * CHUNK]
    kt_s[...] = kt.astype(BF16)
    dwp_s[...] = jnp.zeros_like(dwp_s)
    rc = rc_s[...]
    dw_ref[inner:, :] = jnp.dot(
        jnp.concatenate([qt, -kt], axis=1),
        rc,
        precision=lax.Precision.HIGHEST,
        preferred_element_type=F32,
    )
    db_ref[...] = jnp.sum(rc[:rows], axis=0, keepdims=True)

    def chunk(ch, carry):
        copy(ch).wait()
        base = ch * CHUNK
        dwp = dwp_s[...]
        for i in range(0, CHUNK, 2):
            a = jnp.dot(
                kt_s[...],
                jnp.concatenate([pg[base + i], pg[base + i + 1]], axis=1),
                preferred_element_type=F32,
            )
            dwp = dwp + (
                a[:, :pair] * qt_s[ch, :, i : i + 1] + a[:, pair:] * qt_s[ch, :, i + 1 : i + 2]
            )
        dwp_s[...] = dwp
        return carry

    lax.fori_loop(0, n_chunks, chunk, 0)
    dw_ref[:inner, :] = dwp_s[...]


def _split(x):
    high = x.astype(BF16).astype(F32)
    return high, x - high


def _grad_kernel(
    nq, nk, seq_ref, seqk_ref, gain_ref, beta_ref, dqk_ref, home_ref, dw_ref, db_ref, bp_ref,
    out_ref, dqb_ref, dkb_ref,
):
    me_r = lax.axis_index("row")
    me_c = lax.axis_index("col")
    dq = _unpack(jnp.sum(dqk_ref[pl.ds(me_r * nq, nq)].astype(F32), axis=0))
    dk = home_ref[...]
    for m in range(nk):
        part = _unpack(dqk_ref[m * nq + me_c].astype(F32))
        dk = dk + jnp.where(me_r == m, jnp.zeros_like(part), part)
    dq_b, dk_b = dq.astype(BF16), dk.astype(BF16)
    dqb_ref[...] = dq_b
    dkb_ref[...] = dk_b
    dims = (((0,), (0,)), ((), ()))

    def rows_of(ref, cotangent):
        y = (_norm(ref[...])[0] * gain_ref[...] + beta_ref[...]).astype(BF16)
        return lax.dot_general(y, cotangent, dims, preferred_element_type=F32)

    w_proj = jnp.concatenate([rows_of(seq_ref, dq_b), rows_of(seqk_ref, dk_b)], axis=1)
    n, _, quarter, pair = out_ref.shape
    w_proj = w_proj.reshape(n, 2 * quarter, pair)
    out_ref[:, 0] = w_proj[:, :quarter].astype(BF16)
    out_ref[:, 1] = w_proj[:, quarter:].astype(BF16)
    bp_hi, bp_lo = _split(bp_ref[...])
    place = lax.broadcasted_iota(jnp.int32, (n, quarter, pair), 1)
    last = jnp.broadcast_to(dw_ref[...][:, None, :], place.shape)
    for at, value in enumerate((db_ref[...], bp_hi, bp_lo), 1):
        last = jnp.where(place == at, jnp.broadcast_to(value[None], place.shape), last)
    out_ref[:, 2] = last.astype(BF16)


def _reduce_kernel(x_ref, out_ref, bo_ref, bp_ref):
    total = jnp.sum(x_ref[...].astype(F32), axis=0)
    last = total[2]
    bo_ref[...] = last[1:2]
    bp_ref[...] = last[2:3] + last[3:4]
    w_hi, w_lo = _split(last[0:1])
    last = jnp.concatenate([w_hi, w_lo, jnp.zeros((2, last.shape[1]), F32)], axis=0)
    tile = jnp.concatenate([total[:2], last[None]], axis=0).astype(BF16)
    out_ref[...] = jnp.broadcast_to(tile[None], out_ref.shape)


def _unpack_kernel(x_ref, w_proj_ref, w_out_ref):
    x = x_ref[...].astype(F32)
    w_proj_ref[...] = jnp.concatenate([x[:, 0], x[:, 1]], axis=1).reshape(w_proj_ref.shape)
    w_out_ref[...] = x[:, 2, 0] + x[:, 2, 1]


def _seq_kernel(seq_ref, gain_ref, w_ref, dq_ref, dk_ref, out_ref):
    normed, inverse = _norm(seq_ref[...])
    dqk = jnp.concatenate([dq_ref[...], dk_ref[...]], axis=1)
    dn = (
        lax.dot_general(dqk, w_ref[...], (((1,), (1,)), ((), ())), preferred_element_type=F32)
        * gain_ref[...]
    )
    out_ref[...] = (
        inverse
        * (
            dn
            - jnp.mean(dn, axis=1, keepdims=True)
            - normed * jnp.mean(dn * normed, axis=1, keepdims=True)
        )
    ).astype(BF16)


def local(n_row, n_col, seq, gain, beta, w_proj, b_proj, w_out, pair_grad):
    shard, width = seq.shape
    pair = w_out.shape[1]
    inner = pair // 2
    rows, cols = pair_grad.shape[:2]
    n = n_row * n_col
    nq, nk = rows // shard, cols // shard
    gain = gain.reshape(1, width)
    beta = beta.reshape(1, width)
    shape = jax.ShapeDtypeStruct

    vmem = pl.BlockSpec(memory_space=pltpu.VMEM)
    hbm = pl.BlockSpec(memory_space=pltpu.HBM)
    tile = [pltpu.VMEM(pair_grad.shape, BF16), pltpu.SemaphoreType.DMA((rows // CHUNK,))]

    qk = pl.pallas_call(
        _project_kernel,
        out_shape=shape((n, shard, pair), BF16),
        in_specs=[hbm] * 5,
        out_specs=hbm,
        scratch_shapes=[
            pltpu.VMEM((shard, width), BF16),
            pltpu.VMEM((1, width), F32),
            pltpu.VMEM((1, width), F32),
            pltpu.VMEM((width, pair), BF16),
            pltpu.VMEM((1, pair), F32),
            pltpu.SemaphoreType.DMA((5,)),
            pltpu.VMEM((n // 8, shard, pair), BF16),
            pltpu.SemaphoreType.DMA((8,)),
        ],
        compiler_params=_params(60),
    )(seq, gain, beta, w_proj, b_proj.reshape(1, pair))
    to_sum = [(d, (d % nk) * n_col + d // nk) for d in range(n)]
    to_owner = [(b, a) for a, b in to_sum]
    seq_k = lax.ppermute(seq, BOTH, to_sum)
    qk_all = lax.all_to_all(qk, BOTH, 0, 0, tiled=True)

    rc = pl.pallas_call(
        _totals_kernel,
        out_shape=shape((rows + cols, pair), F32),
        in_specs=[hbm],
        out_specs=hbm,
        scratch_shapes=tile + [pltpu.VMEM((rows + cols, pair), F32), pltpu.SemaphoreType.DMA((1,))],
        compiler_params=_params(60),
        cost_estimate=pl.CostEstimate(
            flops=4 * rows * cols * pair * pair, bytes_accessed=3 * rows * cols * pair, transcendentals=0
        ),
    )(pair_grad)

    own = [pltpu.VMEM((nq, shard, pair), BF16), pltpu.VMEM((nk, shard, pair), BF16)]
    slot = shape((n, shard // 8, 4, pair), BF16)
    dqk_part, home, bp_part = pl.pallas_call(
        functools.partial(_sums_kernel, nq, nk),
        out_shape=(slot, shape((shard, inner), F32), shape((1, pair), F32)),
        in_specs=[hbm] * 5,
        out_specs=(vmem,) * 3,
        scratch_shapes=tile
        + own
        + [
            pltpu.VMEM((pair, pair), BF16),
            pltpu.VMEM((rows + cols, pair), F32),
            pltpu.SemaphoreType.DMA((4,)),
            pltpu.VMEM((2 * pair, pair), BF16),
            pltpu.VMEM((rows, pair), F32),
            pltpu.VMEM((cols // 2, pair), F32),
            pltpu.VMEM((rows, pair), F32),
            pltpu.VMEM((cols // 2, pair), F32),
            pltpu.VMEM((nk, shard, inner), F32),
        ],
        compiler_params=_params(40),
    )(qk_all, pltpu.with_memory_space_constraint(rc, pltpu.HBM), w_out, pair_grad, seq_k)
    dqk_in = lax.all_to_all(dqk_part, BOTH, 0, 0, tiled=True)

    dw_part, db_part = pl.pallas_call(
        _weight_kernel,
        out_shape=(shape((pair, pair), F32), shape((1, pair), F32)),
        in_specs=[hbm] * 3,
        out_specs=(vmem,) * 2,
        scratch_shapes=tile
        + own
        + [
            pltpu.VMEM((rows + cols, pair), F32),
            pltpu.SemaphoreType.DMA((3,)),
            pltpu.VMEM((rows // CHUNK, inner, CHUNK), F32),
            pltpu.VMEM((inner, cols), BF16),
            pltpu.VMEM((inner, pair), F32),
        ],
        compiler_params=_params(40),
        cost_estimate=pl.CostEstimate(
            flops=4 * rows * cols * pair * pair, bytes_accessed=2 * rows * cols * pair, transcendentals=0
        ),
    )(qk_all, rc, pair_grad)

    slots, dq_b, dk_b = pl.pallas_call(
        functools.partial(_grad_kernel, nq, nk),
        out_shape=(slot, shape((shard, inner), BF16), shape((shard, inner), BF16)),
        in_specs=[vmem] * 9,
        out_specs=(vmem,) * 3,
        compiler_params=_params(32),
    )(seq, seq_k, gain, beta, dqk_in, home, dw_part, db_part, bp_part)
    gathered = lax.all_to_all(slots, BOTH, 0, 0, tiled=True)
    dk_own = lax.ppermute(dk_b, BOTH, to_owner)

    reduced, d_b_out, d_b_proj = pl.pallas_call(
        _reduce_kernel,
        out_shape=(slot, shape((1, pair), F32), shape((1, pair), F32)),
        in_specs=[vmem],
        out_specs=(vmem,) * 3,
        compiler_params=_params(32),
    )(gathered)
    spread = lax.all_to_all(reduced, BOTH, 0, 0, tiled=True)

    d_seq = pl.pallas_call(
        _seq_kernel,
        out_shape=shape(seq.shape, BF16),
        in_specs=[vmem] * 5,
        out_specs=vmem,
        compiler_params=_params(32),
    )(seq, gain, w_proj, dq_b, dk_own)

    d_w_proj, d_w_out = pl.pallas_call(
        _unpack_kernel,
        out_shape=(shape((width, pair), F32), shape((pair, pair), F32)),
        in_specs=[vmem],
        out_specs=(vmem,) * 2,
        compiler_params=_params(32),
    )(spread)
    return d_seq, d_w_proj, d_b_proj.reshape(pair), d_w_out, d_b_out.reshape(pair)


def solution(mesh):
    in_specs = (P(BOTH, None), P(), P(), P(), P(), P(), P("row", "col", None))
    out_specs = (P(BOTH, None), P(), P(), P(), P())
    body = functools.partial(local, mesh.shape["row"], mesh.shape["col"])
    return jax.shard_map(body, mesh=mesh, in_specs=in_specs, out_specs=out_specs, check_vma=False)
```

```python
import functools

import jax
import jax.numpy as jnp
from jax import lax
from jax.experimental import pallas as pl
from jax.experimental.pallas import tpu as pltpu
from jax.sharding import PartitionSpec as P

F32 = jnp.float32
BF16 = jnp.bfloat16
BOTH = ("row", "col")
CHUNK = 64


def _params(mib):
    return pltpu.CompilerParams(vmem_limit_bytes=mib * 2**20)


def _norm(seq):
    source = seq.astype(F32)
    centred = source - jnp.mean(source, axis=1, keepdims=True)
    variance = jnp.mean(centred * centred, axis=1, keepdims=True)
    inverse = 1.0 / jnp.sqrt(variance + 1e-05)
    return centred * inverse, inverse


def _start(pairs, sems):
    copies = [pltpu.make_async_copy(a, b, sems.at[n]) for n, (a, b) in enumerate(pairs)]
    for c in copies:
        c.start()
    return copies


def _fetch(pairs, sems):
    for c in _start(pairs, sems):
        c.wait()


def _spread(block_s, out_hbm, sems):
    count = block_s.shape[0]
    parts = range(0, out_hbm.shape[0], count)
    _fetch([(block_s, out_hbm.at[pl.ds(at, count)]) for at in parts], sems)


def _project_kernel(
    seq_hbm, gain_hbm, beta_hbm, w_hbm, b_hbm, out_hbm,
    seq_s, gain_s, beta_s, w_s, b_s, sems, block_s, out_sems,
):
    copies = _start(
        [(seq_hbm, seq_s), (gain_hbm, gain_s), (beta_hbm, beta_s), (w_hbm, w_s), (b_hbm, b_s)],
        sems,
    )
    copies[0].wait()
    normed, _ = _norm(seq_s[...])
    for c in copies[1:]:
        c.wait()
    y = (normed * gain_s[...] + beta_s[...]).astype(BF16)
    qk = (jnp.dot(y, w_s[...], preferred_element_type=F32) + b_s[...]).astype(BF16)
    block_s[...] = jnp.broadcast_to(qk[None], block_s.shape)
    _spread(block_s, out_hbm, out_sems)


def _tile_copies(pg_hbm, pg, sems):
    def copy(ch):
        part = pl.ds(ch * CHUNK, CHUNK)
        return pltpu.make_async_copy(pg_hbm.at[part], pg.at[part], sems.at[ch])

    for ch in range(pg.shape[0] // CHUNK):
        copy(ch).start()
    return copy


def _totals_kernel(pg_hbm, rc_hbm, pg, sems, rc_ref, rc_sem):
    rows, cols, pair = pg.shape
    copy = _tile_copies(pg_hbm, pg, sems)
    over_i = pl.ds(rows, cols)
    rc_ref[over_i] = jnp.zeros((cols, pair), F32)

    def chunk(ch, carry):
        copy(ch).wait()
        base = ch * CHUNK
        total = rc_ref[over_i]
        for i in range(CHUNK):
            block = pg[base + i].astype(F32)
            rc_ref[pl.ds(base + i, 1), :] = jnp.sum(block, axis=0, keepdims=True)
            total = total + block
        rc_ref[over_i] = total
        return carry

    lax.fori_loop(0, rows // CHUNK, chunk, 0)
    _fetch([(rc_ref, rc_hbm)], rc_sem)


def _pack(x):
    n, shard, inner = x.shape
    x = x.reshape(n, shard // 8, 8, inner)
    return jnp.concatenate([x[:, :, :4], x[:, :, 4:]], axis=3)


def _unpack(x):
    inner = x.shape[-1] // 2
    x = jnp.concatenate([x[:, :, :inner], x[:, :, inner:]], axis=1)
    return x.reshape(x.shape[0] * 8, inner)


def _own_slots(qk_hbm, q_s, k_s):
    nq, nk = q_s.shape[0], k_s.shape[0]
    return [
        (qk_hbm.at[pl.ds(lax.axis_index("row") * nq, nq)], q_s),
        (qk_hbm.at[pl.ds(lax.axis_index("col") * nk, nk)], k_s),
    ]


def _own_qk(q_s, k_s):
    nq, shard, pair = q_s.shape
    inner = pair // 2
    q = q_s[...].astype(F32).reshape(nq * shard, pair)[:, :inner]
    k = k_s[...].astype(F32).reshape(k_s.shape[0] * shard, pair)[:, inner:]
    return q, k


def _sums_kernel(
    nq, nk, qk_hbm, rc_hbm, w_hbm, pg_hbm, seqk_hbm, out_ref, home_ref, bp_ref,
    pg, sems, q_s, k_s, w_s, rc_s, in_sems, wbd_s, q2_s, k2_s, dq_s, dk_s, piece_s,
):
    rows, cols, pair = pg.shape
    inner, half = pair // 2, cols // 2
    shard = home_ref.shape[0]
    del seqk_hbm
    small = _start(_own_slots(qk_hbm, q_s, k_s) + [(w_hbm, w_s), (rc_hbm, rc_s)], in_sems)
    copy = _tile_copies(pg_hbm, pg, sems)
    for c in small[:3]:
        c.wait()
    q, k = _own_qk(q_s, k_s)
    q2_s[...] = jnp.concatenate([q, q], axis=1)
    k2_s[...] = jnp.concatenate([k[:half], k[half:]], axis=1)
    wt = w_s[...].astype(F32).T
    blank = jnp.zeros((pair, inner), F32)
    top = jnp.concatenate([wt[:, :inner], blank], axis=1)
    bottom = jnp.concatenate([blank, wt[:, :inner]], axis=1)
    wbd_s[...] = jnp.concatenate([top, bottom], axis=0).astype(BF16)
    dk_s[...] = jnp.zeros_like(dk_s)
    out_ref[...] = jnp.zeros_like(out_ref)

    def chunk(ch, carry):
        copy(ch).wait()
        base = ch * CHUNK
        dk = dk_s[...]
        k2 = k2_s[...]
        for i in range(CHUNK):
            block = pg[base + i]
            g = jnp.dot(
                jnp.concatenate([block[:half], block[half:]], axis=1),
                wbd_s[...],
                preferred_element_type=F32,
            )
            dq_s[pl.ds(base + i, 1), :] = jnp.sum(g * k2, axis=0, keepdims=True)
            dk = dk + g * q2_s[pl.ds(base + i, 1), :]
        dk_s[...] = dk
        return carry

    lax.fori_loop(0, rows // CHUNK, chunk, 0)
    small[3].wait()
    gd = jnp.dot(
        rc_s[...], w_s[...].astype(F32).T[:, inner:], precision=lax.Precision.HIGHEST, preferred_element_type=F32
    )
    dq = dq_s[...]
    dq = dq[:, :inner] + dq[:, inner:] + gd[:rows]
    dk = dk_s[...]
    dk = jnp.concatenate([dk[:, :inner], dk[:, inner:]], axis=0) - gd[rows:]
    bp_ref[...] = jnp.concatenate(
        [jnp.sum(dq, axis=0, keepdims=True), jnp.sum(dk, axis=0, keepdims=True)], axis=1
    )
    me_r = lax.axis_index("row")
    me_c = lax.axis_index("col")
    dk = dk.reshape(nk, shard, inner)
    piece_s[...] = dk
    home_ref[...] = piece_s[me_r]
    packed = _pack(dk).astype(BF16)
    for m in range(nk):
        out_ref[m * nq + me_c] = packed[m]
    out_ref[pl.ds(me_r * nq, nq)] = _pack(dq.reshape(nq, shard, inner)).astype(BF16)


def _weight_kernel(
    qk_hbm, rc_hbm, pg_hbm, dw_ref, db_ref, pg, sems, q_s, k_s, rc_s, in_sems, qt_s, kt_s, dwp_s
):
    rows, cols, pair = pg.shape
    inner = pair // 2
    n_chunks = rows // CHUNK
    copy = _tile_copies(pg_hbm, pg, sems)
    _fetch(_own_slots(qk_hbm, q_s, k_s) + [(rc_hbm, rc_s)], in_sems)
    q, k = _own_qk(q_s, k_s)
    qt, kt = q.T, k.T
    for ch in range(n_chunks):
        qt_s[ch] = qt[:, ch * CHUNK : (ch + 1) * CHUNK]
    kt_s[...] = kt.astype(BF16)
    dwp_s[...] = jnp.zeros_like(dwp_s)
    rc = rc_s[...]
    dw_ref[inner:, :] = jnp.dot(
        jnp.concatenate([qt, -kt], axis=1),
        rc,
        precision=lax.Precision.HIGHEST,
        preferred_element_type=F32,
    )
    db_ref[...] = jnp.sum(rc[:rows], axis=0, keepdims=True)

    def chunk(ch, carry):
        copy(ch).wait()
        base = ch * CHUNK
        dwp = dwp_s[...]
        for i in range(0, CHUNK, 2):
            a = jnp.dot(
                kt_s[...],
                jnp.concatenate([pg[base + i], pg[base + i + 1]], axis=1),
                preferred_element_type=F32,
            )
            dwp = dwp + (
                a[:, :pair] * qt_s[ch, :, i : i + 1] + a[:, pair:] * qt_s[ch, :, i + 1 : i + 2]
            )
        dwp_s[...] = dwp
        return carry

    lax.fori_loop(0, n_chunks, chunk, 0)
    dw_ref[:inner, :] = dwp_s[...]


def _split(x):
    high = x.astype(BF16).astype(F32)
    return high, x - high


def _grad_kernel(
    nq, nk, seq_ref, seqk_ref, gain_ref, beta_ref, dqk_ref, home_ref, dw_ref, db_ref, bp_ref,
    out_ref, dqb_ref, dkb_ref,
):
    me_r = lax.axis_index("row")
    me_c = lax.axis_index("col")
    dq = _unpack(jnp.sum(dqk_ref[pl.ds(me_r * nq, nq)].astype(F32), axis=0))
    dk = home_ref[...]
    for m in range(nk):
        part = _unpack(dqk_ref[m * nq + me_c].astype(F32))
        dk = dk + jnp.where(me_r == m, jnp.zeros_like(part), part)
    dq_b, dk_b = dq.astype(BF16), dk.astype(BF16)
    dqb_ref[...] = dq_b
    dkb_ref[...] = dk_b
    dims = (((0,), (0,)), ((), ()))

    def rows_of(ref, cotangent):
        y = (_norm(ref[...])[0] * gain_ref[...] + beta_ref[...]).astype(BF16)
        return lax.dot_general(y, cotangent, dims, preferred_element_type=F32)

    w_proj = jnp.concatenate([rows_of(seq_ref, dq_b), rows_of(seqk_ref, dk_b)], axis=1)
    n, _, quarter, pair = out_ref.shape
    w_proj = w_proj.reshape(n, 2 * quarter, pair)
    out_ref[:, 0] = w_proj[:, :quarter].astype(BF16)
    out_ref[:, 1] = w_proj[:, quarter:].astype(BF16)
    bp_hi, bp_lo = _split(bp_ref[...])
    place = lax.broadcasted_iota(jnp.int32, (n, quarter, pair), 1)
    last = jnp.broadcast_to(dw_ref[...][:, None, :], place.shape)
    for at, value in enumerate((db_ref[...], bp_hi, bp_lo), 1):
        last = jnp.where(place == at, jnp.broadcast_to(value[None], place.shape), last)
    out_ref[:, 2] = last.astype(BF16)


def _reduce_kernel(x_ref, out_ref, bo_ref, bp_ref):
    total = jnp.sum(x_ref[...].astype(F32), axis=0)
    last = total[2]
    bo_ref[...] = last[1:2]
    bp_ref[...] = last[2:3] + last[3:4]
    pairs = [total[at, row : row + 2] for at in (0, 1) for row in (0, 2)]
    pairs.append(jnp.concatenate(_split(last[0:1]), axis=0))
    tile = jnp.concatenate([p[None] for p in pairs], axis=0).astype(BF16)
    out_ref[...] = jnp.broadcast_to(tile[None], out_ref.shape)


def _unpack_kernel(x_ref, w_proj_ref, w_out_ref):
    x = x_ref[...].astype(F32)
    rows = jnp.concatenate([x[:, at] for at in range(4)], axis=1)
    w_proj_ref[...] = rows.reshape(w_proj_ref.shape)
    w_out_ref[...] = x[:, 4, 0] + x[:, 4, 1]


def _seq_kernel(seq_ref, gain_ref, w_ref, dq_ref, dk_ref, out_ref):
    normed, inverse = _norm(seq_ref[...])
    dqk = jnp.concatenate([dq_ref[...], dk_ref[...]], axis=1)
    dn = (
        lax.dot_general(dqk, w_ref[...], (((1,), (1,)), ((), ())), preferred_element_type=F32)
        * gain_ref[...]
    )
    out_ref[...] = (
        inverse
        * (
            dn
            - jnp.mean(dn, axis=1, keepdims=True)
            - normed * jnp.mean(dn * normed, axis=1, keepdims=True)
        )
    ).astype(BF16)


def local(n_row, n_col, seq, gain, beta, w_proj, b_proj, w_out, pair_grad):
    shard, width = seq.shape
    pair = w_out.shape[1]
    inner = pair // 2
    rows, cols = pair_grad.shape[:2]
    n = n_row * n_col
    nq, nk = rows // shard, cols // shard
    gain = gain.reshape(1, width)
    beta = beta.reshape(1, width)
    shape = jax.ShapeDtypeStruct

    vmem = pl.BlockSpec(memory_space=pltpu.VMEM)
    hbm = pl.BlockSpec(memory_space=pltpu.HBM)
    tile = [pltpu.VMEM(pair_grad.shape, BF16), pltpu.SemaphoreType.DMA((rows // CHUNK,))]

    qk = pl.pallas_call(
        _project_kernel,
        out_shape=shape((n, shard, pair), BF16),
        in_specs=[hbm] * 5,
        out_specs=hbm,
        scratch_shapes=[
            pltpu.VMEM((shard, width), BF16),
            pltpu.VMEM((1, width), F32),
            pltpu.VMEM((1, width), F32),
            pltpu.VMEM((width, pair), BF16),
            pltpu.VMEM((1, pair), F32),
            pltpu.SemaphoreType.DMA((5,)),
            pltpu.VMEM((n // 8, shard, pair), BF16),
            pltpu.SemaphoreType.DMA((8,)),
        ],
        compiler_params=_params(60),
    )(seq, gain, beta, w_proj, b_proj.reshape(1, pair))
    to_sum = [(d, (d % nk) * n_col + d // nk) for d in range(n)]
    to_owner = [(b, a) for a, b in to_sum]
    seq_k = lax.ppermute(seq, BOTH, to_sum)
    qk_all = lax.all_to_all(qk, BOTH, 0, 0, tiled=True)

    rc = pl.pallas_call(
        _totals_kernel,
        out_shape=shape((rows + cols, pair), F32),
        in_specs=[hbm],
        out_specs=hbm,
        scratch_shapes=tile + [pltpu.VMEM((rows + cols, pair), F32), pltpu.SemaphoreType.DMA((1,))],
        compiler_params=_params(60),
        cost_estimate=pl.CostEstimate(
            flops=4 * rows * cols * pair * pair, bytes_accessed=3 * rows * cols * pair, transcendentals=0
        ),
    )(pair_grad)

    own = [pltpu.VMEM((nq, shard, pair), BF16), pltpu.VMEM((nk, shard, pair), BF16)]
    slot = shape((n, shard // 8, 4, pair), BF16)
    dqk_part, home, bp_part = pl.pallas_call(
        functools.partial(_sums_kernel, nq, nk),
        out_shape=(slot, shape((shard, inner), F32), shape((1, pair), F32)),
        in_specs=[hbm] * 5,
        out_specs=(vmem,) * 3,
        scratch_shapes=tile
        + own
        + [
            pltpu.VMEM((pair, pair), BF16),
            pltpu.VMEM((rows + cols, pair), F32),
            pltpu.SemaphoreType.DMA((4,)),
            pltpu.VMEM((2 * pair, pair), BF16),
            pltpu.VMEM((rows, pair), F32),
            pltpu.VMEM((cols // 2, pair), F32),
            pltpu.VMEM((rows, pair), F32),
            pltpu.VMEM((cols // 2, pair), F32),
            pltpu.VMEM((nk, shard, inner), F32),
        ],
        compiler_params=_params(40),
    )(qk_all, pltpu.with_memory_space_constraint(rc, pltpu.HBM), w_out, pair_grad, seq_k)
    dqk_in = lax.all_to_all(dqk_part, BOTH, 0, 0, tiled=True)

    dw_part, db_part = pl.pallas_call(
        _weight_kernel,
        out_shape=(shape((pair, pair), F32), shape((1, pair), F32)),
        in_specs=[hbm] * 3,
        out_specs=(vmem,) * 2,
        scratch_shapes=tile
        + own
        + [
            pltpu.VMEM((rows + cols, pair), F32),
            pltpu.SemaphoreType.DMA((3,)),
            pltpu.VMEM((rows // CHUNK, inner, CHUNK), F32),
            pltpu.VMEM((inner, cols), BF16),
            pltpu.VMEM((inner, pair), F32),
        ],
        compiler_params=_params(40),
        cost_estimate=pl.CostEstimate(
            flops=4 * rows * cols * pair * pair, bytes_accessed=2 * rows * cols * pair, transcendentals=0
        ),
    )(qk_all, rc, pair_grad)

    slots, dq_b, dk_b = pl.pallas_call(
        functools.partial(_grad_kernel, nq, nk),
        out_shape=(slot, shape((shard, inner), BF16), shape((shard, inner), BF16)),
        in_specs=[vmem] * 9,
        out_specs=(vmem,) * 3,
        compiler_params=_params(32),
    )(seq, seq_k, gain, beta, dqk_in, home, dw_part, db_part, bp_part)
    gathered = lax.all_to_all(slots, BOTH, 0, 0, tiled=True)
    dk_own = lax.ppermute(dk_b, BOTH, to_owner)

    reduced, d_b_out, d_b_proj = pl.pallas_call(
        _reduce_kernel,
        out_shape=(shape((n, 5, 2, pair), BF16), shape((1, pair), F32), shape((1, pair), F32)),
        in_specs=[vmem],
        out_specs=(vmem,) * 3,
        compiler_params=_params(32),
    )(gathered)
    spread = lax.all_to_all(reduced, BOTH, 0, 0, tiled=True)

    d_seq = pl.pallas_call(
        _seq_kernel,
        out_shape=shape(seq.shape, BF16),
        in_specs=[vmem] * 5,
        out_specs=vmem,
        compiler_params=_params(32),
    )(seq, gain, w_proj, dq_b, dk_own)

    d_w_proj, d_w_out = pl.pallas_call(
        _unpack_kernel,
        out_shape=(shape((width, pair), F32), shape((pair, pair), F32)),
        in_specs=[vmem],
        out_specs=(vmem,) * 2,
        compiler_params=_params(32),
    )(spread)
    return d_seq, d_w_proj, d_b_proj.reshape(pair), d_w_out, d_b_out.reshape(pair)


def solution(mesh):
    in_specs = (P(BOTH, None), P(), P(), P(), P(), P(), P("row", "col", None))
    out_specs = (P(BOTH, None), P(), P(), P(), P())
    body = functools.partial(local, mesh.shape["row"], mesh.shape["col"])
    return jax.shard_map(body, mesh=mesh, in_specs=in_specs, out_specs=out_specs, check_vma=False)
```

```python
import functools

import jax
import jax.numpy as jnp
from jax import lax
from jax.experimental import pallas as pl
from jax.experimental.pallas import tpu as pltpu
from jax.sharding import PartitionSpec as P

F32 = jnp.float32
BF16 = jnp.bfloat16
BOTH = ("row", "col")
CHUNK = 64


def _params(mib):
    return pltpu.CompilerParams(vmem_limit_bytes=mib * 2**20)


def _norm(seq):
    source = seq.astype(F32)
    centred = source - jnp.mean(source, axis=1, keepdims=True)
    variance = jnp.mean(centred * centred, axis=1, keepdims=True)
    inverse = 1.0 / jnp.sqrt(variance + 1e-05)
    return centred * inverse, inverse


def _start(pairs, sems):
    copies = [pltpu.make_async_copy(a, b, sems.at[n]) for n, (a, b) in enumerate(pairs)]
    for c in copies:
        c.start()
    return copies


def _fetch(pairs, sems):
    for c in _start(pairs, sems):
        c.wait()


def _spread(block_s, out_hbm, sems):
    count = block_s.shape[0]
    parts = range(0, out_hbm.shape[0], count)
    _fetch([(block_s, out_hbm.at[pl.ds(at, count)]) for at in parts], sems)


def _project_kernel(
    seq_hbm, gain_hbm, beta_hbm, w_hbm, b_hbm, out_hbm,
    seq_s, gain_s, beta_s, w_s, b_s, sems, block_s, out_sems,
):
    copies = _start(
        [(seq_hbm, seq_s), (gain_hbm, gain_s), (beta_hbm, beta_s), (w_hbm, w_s), (b_hbm, b_s)],
        sems,
    )
    copies[0].wait()
    normed, _ = _norm(seq_s[...])
    for c in copies[1:]:
        c.wait()
    y = (normed * gain_s[...] + beta_s[...]).astype(BF16)
    qk = (jnp.dot(y, w_s[...], preferred_element_type=F32) + b_s[...]).astype(BF16)
    block_s[...] = jnp.broadcast_to(qk[None], block_s.shape)
    _spread(block_s, out_hbm, out_sems)


def _tile_copies(pg_hbm, pg, sems):
    def copy(ch):
        part = pl.ds(ch * CHUNK, CHUNK)
        return pltpu.make_async_copy(pg_hbm.at[part], pg.at[part], sems.at[ch])

    for ch in range(pg.shape[0] // CHUNK):
        copy(ch).start()
    return copy


def _totals_kernel(pg_hbm, rc_hbm, pg, sems, rc_ref, rc_sem):
    rows, cols, pair = pg.shape
    copy = _tile_copies(pg_hbm, pg, sems)
    over_i = pl.ds(rows, cols)
    rc_ref[over_i] = jnp.zeros((cols, pair), F32)

    def chunk(ch, carry):
        copy(ch).wait()
        base = ch * CHUNK
        total = rc_ref[over_i]
        for i in range(CHUNK):
            block = pg[base + i].astype(F32)
            rc_ref[pl.ds(base + i, 1), :] = jnp.sum(block, axis=0, keepdims=True)
            total = total + block
        rc_ref[over_i] = total
        return carry

    lax.fori_loop(0, rows // CHUNK, chunk, 0)
    _fetch([(rc_ref, rc_hbm)], rc_sem)


def _pack(x):
    n, shard, inner = x.shape
    x = x.reshape(n, shard // 8, 8, inner)
    return jnp.concatenate([x[:, :, :4], x[:, :, 4:]], axis=3)


def _unpack(x):
    inner = x.shape[-1] // 2
    x = jnp.concatenate([x[:, :, :inner], x[:, :, inner:]], axis=1)
    return x.reshape(x.shape[0] * 8, inner)


def _own_slots(qk_hbm, q_s, k_s):
    nq, nk = q_s.shape[0], k_s.shape[0]
    return [
        (qk_hbm.at[pl.ds(lax.axis_index("row") * nq, nq)], q_s),
        (qk_hbm.at[pl.ds(lax.axis_index("col") * nk, nk)], k_s),
    ]


def _own_qk(q_s, k_s):
    nq, shard, pair = q_s.shape
    inner = pair // 2
    q = q_s[...].astype(F32).reshape(nq * shard, pair)[:, :inner]
    k = k_s[...].astype(F32).reshape(k_s.shape[0] * shard, pair)[:, inner:]
    return q, k


def _sums_kernel(
    nq, nk, qk_hbm, rc_hbm, w_hbm, pg_hbm, seqk_hbm, out_ref, home_ref, bp_ref,
    pg, sems, q_s, k_s, w_s, rc_s, in_sems, wbd_s, q2_s, k2_s, dq_s, dk_s, piece_s,
):
    rows, cols, pair = pg.shape
    inner, half = pair // 2, cols // 2
    shard = home_ref.shape[0]
    del seqk_hbm
    small = _start(_own_slots(qk_hbm, q_s, k_s) + [(w_hbm, w_s), (rc_hbm, rc_s)], in_sems)
    copy = _tile_copies(pg_hbm, pg, sems)
    for c in small[:3]:
        c.wait()
    q, k = _own_qk(q_s, k_s)
    q2_s[...] = jnp.concatenate([q, q], axis=1)
    k2_s[...] = jnp.concatenate([k[:half], k[half:]], axis=1)
    wt = w_s[...].astype(F32).T
    blank = jnp.zeros((pair, inner), F32)
    top = jnp.concatenate([wt[:, :inner], blank], axis=1)
    bottom = jnp.concatenate([blank, wt[:, :inner]], axis=1)
    wbd_s[...] = jnp.concatenate([top, bottom], axis=0).astype(BF16)
    dk_s[...] = jnp.zeros_like(dk_s)
    out_ref[...] = jnp.zeros_like(out_ref)

    def chunk(ch, carry):
        copy(ch).wait()
        base = ch * CHUNK
        dk = dk_s[...]
        k2 = k2_s[...]
        for i in range(CHUNK):
            block = pg[base + i]
            g = jnp.dot(
                jnp.concatenate([block[:half], block[half:]], axis=1),
                wbd_s[...],
                preferred_element_type=F32,
            )
            dq_s[pl.ds(base + i, 1), :] = jnp.sum(g * k2, axis=0, keepdims=True)
            dk = dk + g * q2_s[pl.ds(base + i, 1), :]
        dk_s[...] = dk
        return carry

    lax.fori_loop(0, rows // CHUNK, chunk, 0)
    small[3].wait()
    gd = jnp.dot(
        rc_s[...], w_s[...].astype(F32).T[:, inner:], precision=lax.Precision.HIGHEST, preferred_element_type=F32
    )
    dq = dq_s[...]
    dq = dq[:, :inner] + dq[:, inner:] + gd[:rows]
    dk = dk_s[...]
    dk = jnp.concatenate([dk[:, :inner], dk[:, inner:]], axis=0) - gd[rows:]
    bp_ref[...] = jnp.concatenate(
        [jnp.sum(dq, axis=0, keepdims=True), jnp.sum(dk, axis=0, keepdims=True)], axis=1
    )
    me_r = lax.axis_index("row")
    me_c = lax.axis_index("col")
    dk = dk.reshape(nk, shard, inner)
    piece_s[...] = dk
    home_ref[...] = piece_s[me_r]
    packed = _pack(dk).astype(BF16)
    for m in range(nk):
        out_ref[m * nq + me_c] = packed[m]
    out_ref[pl.ds(me_r * nq, nq)] = _pack(dq.reshape(nq, shard, inner)).astype(BF16)


def _weight_kernel(
    qk_hbm, rc_hbm, pg_hbm, dw_ref, db_ref, pg, sems, q_s, k_s, rc_s, in_sems, qt_s, kt_s, dwp_s
):
    rows, cols, pair = pg.shape
    inner = pair // 2
    n_chunks = rows // CHUNK
    copy = _tile_copies(pg_hbm, pg, sems)
    _fetch(_own_slots(qk_hbm, q_s, k_s) + [(rc_hbm, rc_s)], in_sems)
    q, k = _own_qk(q_s, k_s)
    qt, kt = q.T, k.T
    for ch in range(n_chunks):
        qt_s[ch] = qt[:, ch * CHUNK : (ch + 1) * CHUNK]
    kt_s[...] = kt.astype(BF16)
    dwp_s[...] = jnp.zeros_like(dwp_s)
    rc = rc_s[...]
    dw_ref[inner:, :] = jnp.dot(
        jnp.concatenate([qt, -kt], axis=1),
        rc,
        precision=lax.Precision.HIGHEST,
        preferred_element_type=F32,
    )
    db_ref[...] = jnp.sum(rc[:rows], axis=0, keepdims=True)

    def chunk(ch, carry):
        copy(ch).wait()
        base = ch * CHUNK
        dwp = dwp_s[...]
        for i in range(0, CHUNK, 2):
            a = jnp.dot(
                kt_s[...],
                jnp.concatenate([pg[base + i], pg[base + i + 1]], axis=1),
                preferred_element_type=F32,
            )
            dwp = dwp + (
                a[:, :pair] * qt_s[ch, :, i : i + 1] + a[:, pair:] * qt_s[ch, :, i + 1 : i + 2]
            )
        dwp_s[...] = dwp
        return carry

    lax.fori_loop(0, n_chunks, chunk, 0)
    dw_ref[:inner, :] = dwp_s[...]


def _split(x):
    high = x.astype(BF16).astype(F32)
    return high, x - high


def _grad_kernel(
    nq, nk, seq_ref, seqk_ref, gain_ref, beta_ref, dqk_ref, home_ref, dw_ref, db_ref, bp_ref,
    out_ref, dqb_ref, dkb_ref,
):
    me_r = lax.axis_index("row")
    me_c = lax.axis_index("col")
    dq = _unpack(jnp.sum(dqk_ref[pl.ds(me_r * nq, nq)].astype(F32), axis=0))
    dk = home_ref[...]
    for m in range(nk):
        part = _unpack(dqk_ref[m * nq + me_c].astype(F32))
        dk = dk + jnp.where(me_r == m, jnp.zeros_like(part), part)
    dq_b, dk_b = dq.astype(BF16), dk.astype(BF16)
    dqb_ref[...] = dq_b
    dkb_ref[...] = dk_b
    dims = (((0,), (0,)), ((), ()))

    def rows_of(ref, cotangent):
        y = (_norm(ref[...])[0] * gain_ref[...] + beta_ref[...]).astype(BF16)
        return lax.dot_general(y, cotangent, dims, preferred_element_type=F32)

    w_proj = jnp.concatenate([rows_of(seq_ref, dq_b), rows_of(seqk_ref, dk_b)], axis=1)
    n, _, quarter, pair = out_ref.shape
    w_proj = w_proj.reshape(n, 2 * quarter, pair)
    out_ref[:, 0] = w_proj[:, :quarter].astype(BF16)
    out_ref[:, 1] = w_proj[:, quarter:].astype(BF16)
    bp_hi, bp_lo = _split(bp_ref[...])
    place = lax.broadcasted_iota(jnp.int32, (n, quarter, pair), 1)
    last = jnp.broadcast_to(dw_ref[...][:, None, :], place.shape)
    for at, value in enumerate((db_ref[...], bp_hi, bp_lo), 1):
        last = jnp.where(place == at, jnp.broadcast_to(value[None], place.shape), last)
    out_ref[:, 2] = last.astype(BF16)


def _reduce_kernel(x_ref, out_hbm, bo_ref, bp_ref, block_s, out_sems):
    total = jnp.sum(x_ref[...].astype(F32), axis=0)
    last = total[2]
    bo_ref[...] = last[1:2]
    bp_ref[...] = last[2:3] + last[3:4]
    pairs = [total[at, row : row + 2] for at in (0, 1) for row in (0, 2)]
    pairs.append(jnp.concatenate(_split(last[0:1]), axis=0))
    tile = jnp.concatenate([p[None] for p in pairs], axis=0).astype(BF16)
    block_s[...] = jnp.broadcast_to(tile[None], block_s.shape)
    _spread(block_s, out_hbm, out_sems)


def _unpack_kernel(x_ref, w_proj_ref, w_out_ref):
    x = x_ref[...].astype(F32)
    rows = jnp.concatenate([x[:, at] for at in range(4)], axis=1)
    w_proj_ref[...] = rows.reshape(w_proj_ref.shape)
    w_out_ref[...] = x[:, 4, 0] + x[:, 4, 1]


def _seq_kernel(seq_ref, gain_ref, w_ref, dq_ref, dk_ref, out_ref):
    normed, inverse = _norm(seq_ref[...])
    dqk = jnp.concatenate([dq_ref[...], dk_ref[...]], axis=1)
    dn = (
        lax.dot_general(dqk, w_ref[...], (((1,), (1,)), ((), ())), preferred_element_type=F32)
        * gain_ref[...]
    )
    out_ref[...] = (
        inverse
        * (
            dn
            - jnp.mean(dn, axis=1, keepdims=True)
            - normed * jnp.mean(dn * normed, axis=1, keepdims=True)
        )
    ).astype(BF16)


def local(n_row, n_col, seq, gain, beta, w_proj, b_proj, w_out, pair_grad):
    shard, width = seq.shape
    pair = w_out.shape[1]
    inner = pair // 2
    rows, cols = pair_grad.shape[:2]
    n = n_row * n_col
    nq, nk = rows // shard, cols // shard
    gain = gain.reshape(1, width)
    beta = beta.reshape(1, width)
    shape = jax.ShapeDtypeStruct

    vmem = pl.BlockSpec(memory_space=pltpu.VMEM)
    hbm = pl.BlockSpec(memory_space=pltpu.HBM)
    tile = [pltpu.VMEM(pair_grad.shape, BF16), pltpu.SemaphoreType.DMA((rows // CHUNK,))]

    qk = pl.pallas_call(
        _project_kernel,
        out_shape=shape((n, shard, pair), BF16),
        in_specs=[hbm] * 5,
        out_specs=hbm,
        scratch_shapes=[
            pltpu.VMEM((shard, width), BF16),
            pltpu.VMEM((1, width), F32),
            pltpu.VMEM((1, width), F32),
            pltpu.VMEM((width, pair), BF16),
            pltpu.VMEM((1, pair), F32),
            pltpu.SemaphoreType.DMA((5,)),
            pltpu.VMEM((n // 8, shard, pair), BF16),
            pltpu.SemaphoreType.DMA((8,)),
        ],
        compiler_params=_params(60),
    )(seq, gain, beta, w_proj, b_proj.reshape(1, pair))
    to_sum = [(d, (d % nk) * n_col + d // nk) for d in range(n)]
    to_owner = [(b, a) for a, b in to_sum]
    seq_k = lax.ppermute(seq, BOTH, to_sum)
    qk_all = lax.all_to_all(qk, BOTH, 0, 0, tiled=True)

    rc = pl.pallas_call(
        _totals_kernel,
        out_shape=shape((rows + cols, pair), F32),
        in_specs=[hbm],
        out_specs=hbm,
        scratch_shapes=tile + [pltpu.VMEM((rows + cols, pair), F32), pltpu.SemaphoreType.DMA((1,))],
        compiler_params=_params(60),
        cost_estimate=pl.CostEstimate(
            flops=4 * rows * cols * pair * pair, bytes_accessed=3 * rows * cols * pair, transcendentals=0
        ),
    )(pair_grad)

    own = [pltpu.VMEM((nq, shard, pair), BF16), pltpu.VMEM((nk, shard, pair), BF16)]
    slot = shape((n, shard // 8, 4, pair), BF16)
    dqk_part, home, bp_part = pl.pallas_call(
        functools.partial(_sums_kernel, nq, nk),
        out_shape=(slot, shape((shard, inner), F32), shape((1, pair), F32)),
        in_specs=[hbm] * 5,
        out_specs=(vmem,) * 3,
        scratch_shapes=tile
        + own
        + [
            pltpu.VMEM((pair, pair), BF16),
            pltpu.VMEM((rows + cols, pair), F32),
            pltpu.SemaphoreType.DMA((4,)),
            pltpu.VMEM((2 * pair, pair), BF16),
            pltpu.VMEM((rows, pair), F32),
            pltpu.VMEM((cols // 2, pair), F32),
            pltpu.VMEM((rows, pair), F32),
            pltpu.VMEM((cols // 2, pair), F32),
            pltpu.VMEM((nk, shard, inner), F32),
        ],
        compiler_params=_params(40),
    )(qk_all, pltpu.with_memory_space_constraint(rc, pltpu.HBM), w_out, pair_grad, seq_k)
    dqk_in = lax.all_to_all(dqk_part, BOTH, 0, 0, tiled=True)

    dw_part, db_part = pl.pallas_call(
        _weight_kernel,
        out_shape=(shape((pair, pair), F32), shape((1, pair), F32)),
        in_specs=[hbm] * 3,
        out_specs=(vmem,) * 2,
        scratch_shapes=tile
        + own
        + [
            pltpu.VMEM((rows + cols, pair), F32),
            pltpu.SemaphoreType.DMA((3,)),
            pltpu.VMEM((rows // CHUNK, inner, CHUNK), F32),
            pltpu.VMEM((inner, cols), BF16),
            pltpu.VMEM((inner, pair), F32),
        ],
        compiler_params=_params(40),
        cost_estimate=pl.CostEstimate(
            flops=4 * rows * cols * pair * pair, bytes_accessed=2 * rows * cols * pair, transcendentals=0
        ),
    )(qk_all, rc, pair_grad)

    slots, dq_b, dk_b = pl.pallas_call(
        functools.partial(_grad_kernel, nq, nk),
        out_shape=(slot, shape((shard, inner), BF16), shape((shard, inner), BF16)),
        in_specs=[vmem] * 9,
        out_specs=(vmem,) * 3,
        compiler_params=_params(32),
    )(seq, seq_k, gain, beta, dqk_in, home, dw_part, db_part, bp_part)
    gathered = lax.all_to_all(slots, BOTH, 0, 0, tiled=True)
    dk_own = lax.ppermute(dk_b, BOTH, to_owner)

    reduced, d_b_out, d_b_proj = pl.pallas_call(
        _reduce_kernel,
        out_shape=(shape((n, 5, 2, pair), BF16), shape((1, pair), F32), shape((1, pair), F32)),
        in_specs=[vmem],
        out_specs=(hbm, vmem, vmem),
        scratch_shapes=[
            pltpu.VMEM((n // 8, 5, 2, pair), BF16),
            pltpu.SemaphoreType.DMA((8,)),
        ],
        compiler_params=_params(32),
    )(gathered)
    spread = lax.all_to_all(reduced, BOTH, 0, 0, tiled=True)

    d_seq = pl.pallas_call(
        _seq_kernel,
        out_shape=shape(seq.shape, BF16),
        in_specs=[vmem] * 5,
        out_specs=vmem,
        compiler_params=_params(32),
    )(seq, gain, w_proj, dq_b, dk_own)

    d_w_proj, d_w_out = pl.pallas_call(
        _unpack_kernel,
        out_shape=(shape((width, pair), F32), shape((pair, pair), F32)),
        in_specs=[vmem],
        out_specs=(vmem,) * 2,
        compiler_params=_params(32),
    )(spread)
    return d_seq, d_w_proj, d_b_proj.reshape(pair), d_w_out, d_b_out.reshape(pair)


def solution(mesh):
    in_specs = (P(BOTH, None), P(), P(), P(), P(), P(), P("row", "col", None))
    out_specs = (P(BOTH, None), P(), P(), P(), P())
    body = functools.partial(local, mesh.shape["row"], mesh.shape["col"])
    return jax.shard_map(body, mesh=mesh, in_specs=in_specs, out_specs=out_specs, check_vma=False)
```
